128 devices in a mesh: ta: 8 (over x, core), ha: 16 (over y, z).
Axes of the slice: x: 4, y: 4, z: 4, core: 2. Of those that a mesh axis runs over, the one named last changes fastest.
Arguments:
- activations: bfloat16 [16, 32, 160, 512], P('ta', 'ha'), may hold values from -96 to 96
- gain: float32 [512], replicated, may hold values from 0.1 to 1.9
- shift: float32 [512], replicated, may hold values from -3 to 3
- weight: bfloat16 [3, 3, 3, 512, 512], replicated, may hold values from -0.0546875 to 0.0546875
- cotangent: bfloat16 [16, 32, 160, 512], P('ta', 'ha'), may hold values from -8 to 8
Outputs:
- output: bfloat16 [16, 32, 160, 512], P('ta', 'ha')
- input_grad: bfloat16 [16, 32, 160, 512], P('ta', 'ha')
The draws below stay inside these ranges and needn't reach their ends.
All inputs are finite; a program needn't handle non-finite values.
Results may differ from the reference program's by a relative error of at most 0.0049.
Values may be sent and summed in bfloat16 or wider, within the bound.
No kernel may reach another device: no remote copies, remote signals or barrier semaphores. Data moves between devices by JAX's collectives and lax.ppermute only.
A program may use at most 128 MiB of HBM per device.

```python
import math
import jax
import jax.numpy as jnp
from jax import lax

C = 512
GROUPS = 32
W = 160
T_ALL = 16
H_ALL = 32


def draw_activations(key, part):
    key = jax.random.fold_in(key, 1)
    k_base, k_rows, k_chan, k_mean, k_sign = jax.random.split(key, 5)
    shape = (T_ALL, H_ALL, W, C)
    base = jax.random.truncated_normal(k_base, -6.0, 6.0, shape, jnp.float32)
    offset_size = jax.random.uniform(k_mean, (1, 1, 1, C), jnp.float32, 0.5, 1.0)
    row_low = 0.5
    row_scale = jnp.exp((jax.random.uniform(k_rows, (T_ALL, H_ALL, 1, 1), jnp.float32) - 0.5) * math.log(10.0))
    ramp = 0.5 + jnp.arange(T_ALL, dtype=jnp.float32).reshape(T_ALL, 1, 1, 1) / max(T_ALL - 1, 1)
    row_ramp = row_low + jnp.arange(H_ALL, dtype=jnp.float32).reshape(1, H_ALL, 1, 1) / max(H_ALL - 1, 1)
    chan_scale = jnp.exp((jax.random.uniform(k_chan, (1, 1, 1, C), jnp.float32) - 0.5) * math.log(10.0))
    signs = jnp.where(jax.random.bernoulli(k_sign, 0.5, (1, 1, 1, C)), 1.0, -1.0).astype(jnp.float32)
    values = base * row_scale * ramp * chan_scale
    values = values + signs * offset_size * chan_scale * ramp * row_ramp
    return values.astype(jnp.bfloat16)


def draw_cotangent(key, part):
    key = jax.random.fold_in(key, 2)
    k_base, k_bias = jax.random.split(key, 2)
    shape = (T_ALL, H_ALL, W, C)
    base = jax.random.truncated_normal(k_base, -5.0, 5.0, shape, jnp.float32)
    bias = 0.8 * jax.random.truncated_normal(k_bias, -3.0, 3.0, (C,), jnp.float32)
    values = base + bias.reshape(1, 1, 1, C)
    return values.astype(jnp.bfloat16)


def noise(key, extent, spread, reach, kind=jnp.bfloat16):
    drawn = jax.random.normal(key, extent, jnp.float32) * spread
    return jnp.minimum(jnp.maximum(drawn, -reach), reach).astype(kind)


def setup_inputs(seed: int = 0) -> dict:
    key_list = jax.random.split(jax.random.key(seed), 6)
    activations = draw_activations(jax.random.fold_in(key_list[5], 71), 0)
    gain = jnp.clip(1.0 + 0.18 * jax.random.normal(key_list[1], (C,), jnp.float32), 0.1, 1.9)
    shift = noise(key_list[2], (C,), 0.5, 3.0, jnp.float32)
    weight = noise(key_list[3], (3, 3, 3, C, C), (27 * C) ** -0.5, 0.0546875)
    cotangent = draw_cotangent(jax.random.fold_in(key_list[5], 71), 0)
    return {"activations": activations, "gain": gain, "shift": shift, "weight": weight, "cotangent": cotangent}


def group_sum(values, groups):
    per_channel = lax.optimization_barrier(jnp.sum(values.reshape(-1, values.shape[-1]), axis=0))
    return lax.optimization_barrier(jnp.sum(per_channel.reshape(groups, -1), axis=1))

def reference(activations, gain, shift, weight, cotangent):
    frames, rows, cols, chans = activations.shape
    per_group = chans // GROUPS
    count = frames * rows * cols * per_group
    xf = activations.astype(jnp.float32)
    mean = group_sum(xf, GROUPS) / count
    mean_c = jnp.repeat(mean, per_group)
    centered = xf - mean_c
    var = group_sum(centered * centered, GROUPS) / count
    rstd_c = jnp.repeat(lax.rsqrt(var + 1e-06), per_group)
    normed = centered * rstd_c
    pre = normed * gain + shift
    acts = jax.nn.silu(pre).astype(jnp.bfloat16)
    padded = jnp.concatenate([acts[:1], acts[:1], acts], axis=0)
    padded = jnp.pad(padded, ((0, 0), (1, 1), (1, 1), (0, 0)))
    total = jnp.zeros((frames * rows * cols, chans), jnp.float32)
    for a in range(3):
        for b in range(3):
            for c in range(3):
                piece = padded[a:a + frames, b:b + rows, c:c + cols].reshape(-1, chans)
                total = total + jnp.dot(piece, weight[a, b, c], preferred_element_type=jnp.float32)
    output = total.reshape(frames, rows, cols, chans).astype(jnp.bfloat16)
    flat_cot = cotangent.reshape(-1, chans)
    padded_grad = jnp.zeros((frames + 2, rows + 2, cols + 2, chans), jnp.float32)
    for a in range(3):
        for b in range(3):
            for c in range(3):
                term = jnp.dot(flat_cot, weight[a, b, c].T, preferred_element_type=jnp.float32)
                padded_grad = padded_grad.at[a:a + frames, b:b + rows, c:c + cols].add(term.reshape(frames, rows, cols, chans))
    inner = padded_grad[:, 1:-1, 1:-1]
    acts_grad = inner[2:]
    acts_grad = acts_grad.at[0].add(inner[0] + inner[1])
    sig = jax.nn.sigmoid(pre)
    pre_grad = acts_grad * sig * (1.0 + pre * (1.0 - sig))
    shift_sum = lax.optimization_barrier(jnp.sum(pre_grad.reshape(-1, chans), axis=0))
    gain_sum = lax.optimization_barrier(jnp.sum((pre_grad * normed).reshape(-1, chans), axis=0))
    first = jnp.repeat(lax.optimization_barrier(jnp.sum((gain * shift_sum).reshape(GROUPS, -1), axis=1)) / count, per_group)
    second = jnp.repeat(lax.optimization_barrier(jnp.sum((gain * gain_sum).reshape(GROUPS, -1), axis=1)) / count, per_group)
    input_grad = (rstd_c * (pre_grad * gain - first - normed * second)).astype(jnp.bfloat16)
    return (output, input_grad)
```

```python
import jax
import jax.numpy as jnp
from jax import lax
from jax.experimental import pallas as pl
from jax.experimental.pallas import tpu as pltpu
from jax.sharding import PartitionSpec as P

GROUPS = 32
LANES = 128
F32 = jnp.float32
BF16 = jnp.bfloat16
ANY = pl.BlockSpec(memory_space=pl.ANY)
WHOLE = pl.BlockSpec(memory_space=pltpu.VMEM)
DMA = pltpu.SemaphoreType.DMA
BOTH = ("ta", "ha")


def params(mebibytes):
    return pltpu.CompilerParams(vmem_limit_bytes=mebibytes * 2**20)


def member(chans, offset, across):
    shape, chan_dim = ((LANES, chans), 1) if across else ((chans, LANES), 0)
    per_group = chans // GROUPS
    chan = lax.broadcasted_iota(jnp.int32, shape, chan_dim)
    lane = lax.broadcasted_iota(jnp.int32, shape, 1 - chan_dim) - offset
    inside = (chan >= lane * per_group) & (chan < (lane + 1) * per_group)
    return jnp.where(inside & (lane >= 0) & (lane < GROUPS), 1.0, 0.0).astype(F32)


def exact_dot(left, right):
    return jnp.dot(left, right, precision=lax.Precision.HIGHEST, preferred_element_type=F32)


def to_groups(by_chan, offset):
    lanes = exact_dot(by_chan, member(by_chan.shape[1], offset, False))
    return jnp.sum(lanes, axis=0, keepdims=True)


def to_chans(by_group, chans, offset):
    rows = jnp.broadcast_to(by_group, (8, LANES))
    return exact_dot(rows, member(chans, offset, True))


def eights(value):
    return value.reshape(value.shape[0] // 8, 8, value.shape[1])


def stats_kernel(act, cot, pay, up, down, block, load_sem, pack_sem):
    frames, rows, cols, chans = block.shape
    load = pltpu.make_async_copy(act, block, load_sem)
    load.start()
    packs = []
    for i, source in enumerate((act, cot)):
        packs.append(pltpu.make_async_copy(source.at[:, rows - 1], up.at[i], pack_sem.at[2 * i]))
        packs.append(pltpu.make_async_copy(source.at[:, 0], down.at[i], pack_sem.at[2 * i + 1]))
    for pack in packs:
        pack.start()
    load.wait()
    entries = frames * rows * cols * (chans // GROUPS)
    total = jnp.zeros((8, chans), F32)
    for t in range(frames):
        for h in range(rows):
            total = total + jnp.sum(eights(block[t, h].astype(F32)), axis=0)
    sums = to_groups(total, 0)
    mean = to_chans(sums / entries, chans, 0)
    spread = jnp.zeros((8, chans), F32)
    for t in range(frames):
        for h in range(rows):
            centered = eights(block[t, h].astype(F32)) - mean[None]
            spread = spread + jnp.sum(centered * centered, axis=0)
    row = sums + to_groups(spread, GROUPS)
    pay[...] = jnp.broadcast_to(row, pay.shape)
    for pack in packs:
        pack.wait()


def grad_kernel(full, part, source, target, pack_act, *refs):
    if pack_act:
        cot, above, below, weight, act, out, longer, ext, taps, acc, ext_sem, tap_sem, act_sem = refs
    else:
        cot, above, below, weight, out, ext, taps, acc, ext_sem, tap_sem = refs
    rows, cols, chans = cot.shape[1:]
    loads = [
        pltpu.make_async_copy(cot, ext.at[:, 1 : rows + 1], ext_sem.at[0]),
        pltpu.make_async_copy(above.at[1], ext.at[:, 0], ext_sem.at[1]),
        pltpu.make_async_copy(below.at[1], ext.at[:, rows + 1], ext_sem.at[2]),
    ]
    for load in loads:
        load.start()
    order = [(k, b) for k in range(2) for b in range(3)]
    fetches = []
    for n, (k, b) in enumerate(order):
        fetches.append(pltpu.make_async_copy(weight.at[(full, part)[k], b], taps.at[n], tap_sem.at[n]))
        fetches[-1].start()
    packs = []
    if pack_act:
        packs = [
            pltpu.make_async_copy(act, longer.at[:, 1 : rows + 1], act_sem.at[0]),
            pltpu.make_async_copy(above.at[0], longer.at[:, 0], act_sem.at[1]),
            pltpu.make_async_copy(below.at[0], longer.at[:, rows + 1], act_sem.at[2]),
        ]
        for pack in packs:
            pack.start()
    for load in loads:
        load.wait()
    half = rows * cols
    for n, (k, b) in enumerate(order):
        fetches[n].wait()
        if k == 0:
            left = ext[:, 2 - b : 2 - b + rows].reshape(2 * half, chans)
            where = slice(0, 2 * half)
        else:
            left = ext[source, 2 - b : 2 - b + rows].reshape(half, chans)
            where = slice(target * half, (target + 1) * half)
        for c in range(3):
            term = lax.dot_general(
                left, taps[n, c], (((1,), (1,)), ((), ())), preferred_element_type=F32
            )
            if n == 0:
                acc[c, where] = term
            else:
                acc[c, where] += term
    combine(acc, out, 2, 0)
    for pack in packs:
        pack.wait()


def combine(acc, out, earlier, later):
    frames, rows, cols, chans = out.shape
    col = lax.broadcasted_iota(jnp.int32, (cols, chans), 0)
    for t in range(frames):
        for h in range(rows):
            at = slice((t * rows + h) * cols, (t * rows + h + 1) * cols)
            before = jnp.where(col == 0, 0.0, pltpu.roll(acc[earlier, at], 1, 0))
            after = jnp.where(col == cols - 1, 0.0, pltpu.roll(acc[later, at], cols - 1, 0))
            out[t, h] = (before + acc[1, at] + after).astype(out.dtype)


def group_stats(gathered, entries, chans):
    parts = gathered.shape[0]
    count = parts * entries
    sums = jnp.sum(gathered, axis=0, keepdims=True)
    mean = sums / count
    apart = gathered * (1.0 / entries) - mean
    between = jnp.sum(apart * apart, axis=0, keepdims=True) * entries
    spread = to_chans(between, chans, 0) + to_chans(sums, chans, GROUPS)
    return to_chans(mean, chans, 0), lax.rsqrt(spread / count + 1e-06)


def point_kernel(own, incoming, early, act, gathered, gain, shift, pre_grad, pay, stats):
    frames, rows, cols, chans = act.shape
    entries = frames * rows * cols * (chans // GROUPS)
    mean, rstd = group_stats(gathered[...], entries, chans)
    stats[0] = mean
    stats[1] = rstd
    first = lax.axis_index("ta") == 0
    scale = jnp.where(first, 1.0, 0.0).astype(F32)
    gains = jnp.broadcast_to(gain[...], (8, chans))
    shifts = jnp.broadcast_to(shift[...], (8, chans))
    shift_sum = jnp.zeros((8, chans), F32)
    gain_sum = jnp.zeros((8, chans), F32)
    for t in range(frames):
        for h in range(rows):
            grad = own[t, h] + incoming[t, h].astype(F32)
            if t == 0:
                grad = grad + scale * (early[0, h].astype(F32) + early[1, h].astype(F32))
            normed = (eights(act[t, h].astype(F32)) - mean[None]) * rstd[None]
            pre = normed * gains[None] + shifts[None]
            sig = 1.0 / (1.0 + jnp.exp(-pre))
            local = eights(grad) * sig * (1.0 + pre * (1.0 - sig))
            pre_grad[t, h] = local.reshape(cols, chans)
            shift_sum = shift_sum + jnp.sum(local, axis=0)
            gain_sum = gain_sum + jnp.sum(local * normed, axis=0)
    row = to_groups(gains * shift_sum, 0) + to_groups(gains * gain_sum, GROUPS)
    pay[...] = jnp.broadcast_to(row, pay.shape)


def conv_kernel(act, above, below, prior, weight, stats, gain, shift, out, raw, ext, taps, acc, raw_sem, tap_sem):
    frames, rows, cols, chans = act.shape
    first = lax.axis_index("ta") == 0
    loads = [
        pltpu.make_async_copy(act, raw.at[2:4, 1 : rows + 1], raw_sem.at[0]),
        pltpu.make_async_copy(above.at[0], raw.at[2:4, 0], raw_sem.at[1]),
        pltpu.make_async_copy(below.at[0], raw.at[2:4, rows + 1], raw_sem.at[2]),
        pltpu.make_async_copy(prior, raw.at[0:2], raw_sem.at[3]),
    ]
    for load in loads:
        load.start()
    order = [(a, b) for a in (2, 1, 0) for b in range(3)]
    fetches = []
    for n, (a, b) in enumerate(order):
        fetches.append(pltpu.make_async_copy(weight.at[a, b], taps.at[n], tap_sem.at[n]))
        fetches[-1].start()
    for load in loads:
        load.wait()
    mean, rstd = stats[0], stats[1]
    gains = jnp.broadcast_to(gain[...], (8, chans))
    shifts = jnp.broadcast_to(shift[...], (8, chans))
    row_at = lax.axis_index("ha")
    last_row = lax.axis_size("ha") - 1

    def activate(t, i):
        normed = (eights(raw[t, i].astype(F32)) - mean[None]) * rstd[None]
        pre = normed * gains[None] + shifts[None]
        value = pre / (1.0 + jnp.exp(-pre))
        if i == 0:
            value = value * jnp.where(row_at == 0, 0.0, 1.0)
        if i == rows + 1:
            value = value * jnp.where(row_at == last_row, 0.0, 1.0)
        ext[t, i] = value.reshape(cols, chans).astype(BF16)

    for t in (2, 3, 0, 1):
        for i in range(rows + 2):
            activate(t, i)

    @pl.when(first)
    def _():
        ext[0] = ext[2]
        ext[1] = ext[2]

    for n, (a, b) in enumerate(order):
        fetches[n].wait()
        left = ext[a : a + frames, b : b + rows].reshape(frames * rows * cols, chans)
        for c in range(3):
            term = jnp.dot(left, taps[n, c], preferred_element_type=F32)
            if n == 0:
                acc[c] = term
            else:
                acc[c] += term
    combine(acc, out, 0, 2)


def final_kernel(pre_grad, act, gathered, stats, gain, out):
    frames, rows, cols, chans = act.shape
    count = gathered.shape[0] * frames * rows * cols * (chans // GROUPS)
    sums = jnp.sum(gathered[...], axis=0, keepdims=True) / count
    first = to_chans(sums, chans, 0)
    second = to_chans(sums, chans, GROUPS)
    mean, rstd = stats[0], stats[1]
    gains = jnp.broadcast_to(gain[...], (8, chans))
    for t in range(frames):
        for h in range(rows):
            normed = (eights(act[t, h].astype(F32)) - mean[None]) * rstd[None]
            value = rstd[None] * (eights(pre_grad[t, h]) * gains[None] - first[None] - normed * second[None])
            out[t, h] = value.reshape(cols, chans).astype(BF16)


def moved(value, frame_step, row_step):
    frames, rows = lax.axis_size("ta"), lax.axis_size("ha")
    pairs = []
    for t in range(frames):
        for h in range(rows):
            to_t, to_h = t + frame_step, h + row_step
            if 0 <= to_t < frames and 0 <= to_h < rows:
                pairs.append((t * rows + h, to_t * rows + to_h))
    return lax.ppermute(value, BOTH, pairs)


def on_device(activations, gain, shift, weight, cotangent):
    shape = activations.shape
    frames, rows, cols, chans = shape
    parts = lax.axis_size("ta") * lax.axis_size("ha")
    gain, shift = gain.reshape(1, chans), shift.reshape(1, chans)
    gathered_shape = jax.ShapeDtypeStruct((parts, LANES), F32)
    edge = jax.ShapeDtypeStruct((2, frames, cols, chans), BF16)
    longer_shape = (frames, rows + 2, cols, chans)
    positions = frames * rows * cols

    pay, up, down = pl.pallas_call(
        stats_kernel,
        in_specs=[ANY, ANY],
        out_specs=[WHOLE, ANY, ANY],
        out_shape=[gathered_shape, edge, edge],
        scratch_shapes=[pltpu.VMEM(shape, BF16), DMA, DMA((4,))],
        compiler_params=params(16),
    )(activations, cotangent)
    above = moved(up, 0, 1)
    below = moved(down, 0, -1)
    gathered = lax.all_to_all(pay, BOTH, 0, 0, tiled=True)

    def grad_scratch():
        return [
            pltpu.VMEM(longer_shape, BF16),
            pltpu.VMEM((6, 3, chans, chans), BF16),
            pltpu.VMEM((3, positions, chans), F32),
            DMA((3,)),
            DMA((6,)),
        ]

    early, longer = pl.pallas_call(
        lambda *refs: grad_kernel(0, 1, 0, 1, True, *refs),
        in_specs=[ANY] * 5,
        out_specs=[WHOLE, ANY],
        out_shape=[jax.ShapeDtypeStruct(shape, BF16), jax.ShapeDtypeStruct(longer_shape, BF16)],
        scratch_shapes=grad_scratch() + [DMA((3,))],
        compiler_params=params(32),
    )(cotangent, above, below, weight, activations)
    incoming = moved(early, -1, 0)
    prior = moved(longer, 1, 0)
    own = pl.pallas_call(
        lambda *refs: grad_kernel(2, 1, 1, 0, False, *refs),
        in_specs=[ANY] * 4,
        out_specs=WHOLE,
        out_shape=jax.ShapeDtypeStruct(shape, F32),
        scratch_shapes=grad_scratch(),
        compiler_params=params(32),
    )(cotangent, above, below, weight)
    pre_grad, pay, stats = pl.pallas_call(
        point_kernel,
        in_specs=[WHOLE] * 7,
        out_specs=[WHOLE] * 3,
        out_shape=[
            jax.ShapeDtypeStruct(shape, F32),
            gathered_shape,
            jax.ShapeDtypeStruct((2, 8, chans), F32),
        ],
        compiler_params=params(32),
    )(own, incoming, early, activations, gathered, gain, shift)
    gathered = lax.all_to_all(pay, BOTH, 0, 0, tiled=True)
    output = pl.pallas_call(
        conv_kernel,
        in_specs=[ANY] * 5 + [WHOLE] * 3,
        out_specs=WHOLE,
        out_shape=jax.ShapeDtypeStruct(shape, BF16),
        scratch_shapes=[
            pltpu.VMEM((frames + 2, rows + 2, cols, chans), BF16),
            pltpu.VMEM((frames + 2, rows + 2, cols, chans), BF16),
            pltpu.VMEM((9, 3, chans, chans), BF16),
            pltpu.VMEM((3, positions, chans), F32),
            DMA((4,)),
            DMA((9,)),
        ],
        compiler_params=params(44),
    )(activations, above, below, prior, weight, stats, gain, shift)
    input_grad = pl.pallas_call(
        final_kernel,
        in_specs=[WHOLE] * 5,
        out_specs=WHOLE,
        out_shape=jax.ShapeDtypeStruct(shape, BF16),
        compiler_params=params(32),
    )(pre_grad, activations, gathered, stats, gain)
    return (output, input_grad)


def solution(mesh):
    placed = (P("ta", "ha", None, None), P(), P(), P(), P("ta", "ha", None, None))
    return jax.shard_map(
        on_device,
        mesh=mesh,
        in_specs=placed,
        out_specs=(P("ta", "ha", None, None), P("ta", "ha", None, None)),
        check_vma=False,
    )
```

```python
import jax
import jax.numpy as jnp
from jax import lax
from jax.experimental import pallas as pl
from jax.experimental.pallas import tpu as pltpu
from jax.sharding import PartitionSpec as P

GROUPS = 32
LANES = 128
F32 = jnp.float32
BF16 = jnp.bfloat16
HBM = pl.BlockSpec(memory_space=pltpu.HBM)
WHOLE = pl.BlockSpec(memory_space=pltpu.VMEM)
DMA = pltpu.SemaphoreType.DMA
BOTH = ("ta", "ha")


def params(mebibytes):
    return pltpu.CompilerParams(vmem_limit_bytes=mebibytes * 2**20)


def member(chans, offset, across):
    shape, chan_dim = ((LANES, chans), 1) if across else ((chans, LANES), 0)
    per_group = chans // GROUPS
    chan = lax.broadcasted_iota(jnp.int32, shape, chan_dim)
    lane = lax.broadcasted_iota(jnp.int32, shape, 1 - chan_dim) - offset
    inside = (chan >= lane * per_group) & (chan < (lane + 1) * per_group)
    return jnp.where(inside & (lane >= 0) & (lane < GROUPS), 1.0, 0.0).astype(F32)


def exact_dot(left, right):
    return jnp.dot(left, right, precision=lax.Precision.HIGHEST, preferred_element_type=F32)


def to_groups(by_chan, offset):
    lanes = exact_dot(by_chan, member(by_chan.shape[1], offset, False))
    return jnp.sum(lanes, axis=0, keepdims=True)


def to_chans(by_group, chans, offset):
    rows = jnp.broadcast_to(by_group, (8, LANES))
    return exact_dot(rows, member(chans, offset, True))


def eights(value):
    return value.reshape(value.shape[0] // 8, 8, value.shape[1])


def stats_kernel(act, cot, pay, up, down, block, load_sem, pack_sem):
    frames, rows, cols, chans = block.shape
    load = pltpu.make_async_copy(act, block, load_sem)
    load.start()
    packs = []
    for i, source in enumerate((act, cot)):
        packs.append(pltpu.make_async_copy(source.at[:, rows - 1], up.at[i], pack_sem.at[2 * i]))
        packs.append(pltpu.make_async_copy(source.at[:, 0], down.at[i], pack_sem.at[2 * i + 1]))
    for pack in packs:
        pack.start()
    load.wait()
    entries = frames * rows * cols * (chans // GROUPS)
    total = jnp.zeros((8, chans), F32)
    for t in range(frames):
        for h in range(rows):
            total = total + jnp.sum(eights(block[t, h].astype(F32)), axis=0)
    sums = to_groups(total, 0)
    mean = to_chans(sums / entries, chans, 0)
    spread = jnp.zeros((8, chans), F32)
    for t in range(frames):
        for h in range(rows):
            centered = eights(block[t, h].astype(F32)) - mean[None]
            spread = spread + jnp.sum(centered * centered, axis=0)
    row = sums + to_groups(spread, GROUPS)
    pay[...] = jnp.broadcast_to(row, pay.shape)
    for pack in packs:
        pack.wait()


def grad_kernel(full, part, source, target, pack_act, *refs):
    if pack_act:
        cot, above, below, weight, act, out, longer, ext, taps, acc, ext_sem, tap_sem, act_sem = refs
    else:
        cot, above, below, weight, out, ext, taps, acc, ext_sem, tap_sem = refs
    rows, cols, chans = cot.shape[1:]
    loads = [
        pltpu.make_async_copy(cot, ext.at[:, 1 : rows + 1], ext_sem.at[0]),
        pltpu.make_async_copy(above.at[1], ext.at[:, 0], ext_sem.at[1]),
        pltpu.make_async_copy(below.at[1], ext.at[:, rows + 1], ext_sem.at[2]),
    ]
    for load in loads:
        load.start()
    order = [(k, b) for k in range(2) for b in range(3)]
    fetches = []
    for n, (k, b) in enumerate(order):
        fetches.append(pltpu.make_async_copy(weight.at[(full, part)[k], b], taps.at[n], tap_sem.at[n]))
        fetches[-1].start()
    packs = []
    if pack_act:
        packs = [
            pltpu.make_async_copy(act, longer.at[:, 1 : rows + 1], act_sem.at[0]),
            pltpu.make_async_copy(above.at[0], longer.at[:, 0], act_sem.at[1]),
            pltpu.make_async_copy(below.at[0], longer.at[:, rows + 1], act_sem.at[2]),
        ]
        for pack in packs:
            pack.start()
    for load in loads:
        load.wait()
    half = rows * cols
    for n, (k, b) in enumerate(order):
        fetches[n].wait()
        if k == 0:
            left = ext[:, 2 - b : 2 - b + rows].reshape(2 * half, chans)
            where = slice(0, 2 * half)
        else:
            left = ext[source, 2 - b : 2 - b + rows].reshape(half, chans)
            where = slice(target * half, (target + 1) * half)
        for c in range(3):
            term = lax.dot_general(
                left, taps[n, c], (((1,), (1,)), ((), ())), preferred_element_type=F32
            )
            if n == 0:
                acc[c, where] = term
            else:
                acc[c, where] += term
    combine(acc, out, 2, 0)
    for pack in packs:
        pack.wait()


def combine(acc, out, earlier, later):
    frames, rows, cols, chans = out.shape
    col = lax.broadcasted_iota(jnp.int32, (cols, chans), 0)
    for t in range(frames):
        for h in range(rows):
            at = slice((t * rows + h) * cols, (t * rows + h + 1) * cols)
            before = jnp.where(col == 0, 0.0, pltpu.roll(acc[earlier, at], 1, 0))
            after = jnp.where(col == cols - 1, 0.0, pltpu.roll(acc[later, at], cols - 1, 0))
            out[t, h] = (before + acc[1, at] + after).astype(out.dtype)


def group_stats(gathered, entries, chans):
    parts = gathered.shape[0]
    count = parts * entries
    sums = jnp.sum(gathered, axis=0, keepdims=True)
    mean = sums / count
    apart = gathered * (1.0 / entries) - mean
    between = jnp.sum(apart * apart, axis=0, keepdims=True) * entries
    spread = to_chans(between, chans, 0) + to_chans(sums, chans, GROUPS)
    return to_chans(mean, chans, 0), lax.rsqrt(spread / count + 1e-06)


def point_kernel(own, incoming, early, act, gathered, gain, shift, pre_grad, pay, stats):
    frames, rows, cols, chans = act.shape
    entries = frames * rows * cols * (chans // GROUPS)
    mean, rstd = group_stats(gathered[...], entries, chans)
    stats[0] = mean
    stats[1] = rstd
    first = lax.axis_index("ta") == 0
    scale = jnp.where(first, 1.0, 0.0).astype(F32)
    gains = jnp.broadcast_to(gain[...], (8, chans))
    shifts = jnp.broadcast_to(shift[...], (8, chans))
    shift_sum = jnp.zeros((8, chans), F32)
    gain_sum = jnp.zeros((8, chans), F32)
    for t in range(frames):
        for h in range(rows):
            grad = own[t, h] + incoming[t, h].astype(F32)
            if t == 0:
                grad = grad + scale * (early[0, h].astype(F32) + early[1, h].astype(F32))
            normed = (eights(act[t, h].astype(F32)) - mean[None]) * rstd[None]
            pre = normed * gains[None] + shifts[None]
            sig = 1.0 / (1.0 + jnp.exp(-pre))
            local = eights(grad) * sig * (1.0 + pre * (1.0 - sig))
            pre_grad[t, h] = local.reshape(cols, chans)
            shift_sum = shift_sum + jnp.sum(local, axis=0)
            gain_sum = gain_sum + jnp.sum(local * normed, axis=0)
    row = to_groups(gains * shift_sum, 0) + to_groups(gains * gain_sum, GROUPS)
    pay[...] = jnp.broadcast_to(row, pay.shape)


def conv_kernel(act, above, below, prior, weight, stats, gain, shift, out, raw, ext, taps, acc, raw_sem, tap_sem):
    frames, rows, cols, chans = act.shape
    first = lax.axis_index("ta") == 0
    loads = [
        pltpu.make_async_copy(act, raw.at[2:4, 1 : rows + 1], raw_sem.at[0]),
        pltpu.make_async_copy(above.at[0], raw.at[2:4, 0], raw_sem.at[1]),
        pltpu.make_async_copy(below.at[0], raw.at[2:4, rows + 1], raw_sem.at[2]),
        pltpu.make_async_copy(prior, raw.at[0:2], raw_sem.at[3]),
    ]
    for load in loads:
        load.start()
    order = [(a, b) for a in (2, 1, 0) for b in range(3)]
    fetches = []
    for n, (a, b) in enumerate(order):
        fetches.append(pltpu.make_async_copy(weight.at[a, b], taps.at[n], tap_sem.at[n]))
        fetches[-1].start()
    for load in loads:
        load.wait()
    mean, rstd = stats[0], stats[1]
    gains = jnp.broadcast_to(gain[...], (8, chans))
    shifts = jnp.broadcast_to(shift[...], (8, chans))
    row_at = lax.axis_index("ha")
    last_row = lax.axis_size("ha") - 1

    def activate(t, i):
        normed = (eights(raw[t, i].astype(F32)) - mean[None]) * rstd[None]
        pre = normed * gains[None] + shifts[None]
        value = pre / (1.0 + jnp.exp(-pre))
        if i == 0:
            value = value * jnp.where(row_at == 0, 0.0, 1.0)
        if i == rows + 1:
            value = value * jnp.where(row_at == last_row, 0.0, 1.0)
        ext[t, i] = value.reshape(cols, chans).astype(BF16)

    for t in (2, 3, 0, 1):
        for i in range(rows + 2):
            activate(t, i)

    @pl.when(first)
    def _():
        ext[0] = ext[2]
        ext[1] = ext[2]

    for n, (a, b) in enumerate(order):
        fetches[n].wait()
        left = ext[a : a + frames, b : b + rows].reshape(frames * rows * cols, chans)
        for c in range(3):
            term = jnp.dot(left, taps[n, c], preferred_element_type=F32)
            if n == 0:
                acc[c] = term
            else:
                acc[c] += term
    combine(acc, out, 0, 2)


def final_kernel(pre_grad, act, gathered, stats, gain, out):
    frames, rows, cols, chans = act.shape
    count = gathered.shape[0] * frames * rows * cols * (chans // GROUPS)
    sums = jnp.sum(gathered[...], axis=0, keepdims=True) / count
    first = to_chans(sums, chans, 0)
    second = to_chans(sums, chans, GROUPS)
    mean, rstd = stats[0], stats[1]
    gains = jnp.broadcast_to(gain[...], (8, chans))
    for t in range(frames):
        for h in range(rows):
            normed = (eights(act[t, h].astype(F32)) - mean[None]) * rstd[None]
            value = rstd[None] * (eights(pre_grad[t, h]) * gains[None] - first[None] - normed * second[None])
            out[t, h] = value.reshape(cols, chans).astype(BF16)


def moved(value, frame_step, row_step):
    frames, rows = lax.axis_size("ta"), lax.axis_size("ha")
    pairs = []
    for t in range(frames):
        for h in range(rows):
            to_t, to_h = t + frame_step, h + row_step
            if 0 <= to_t < frames and 0 <= to_h < rows:
                pairs.append((t * rows + h, to_t * rows + to_h))
    return lax.ppermute(value, BOTH, pairs)


def in_hbm(value):
    return pltpu.with_memory_space_constraint(value, pltpu.HBM)


def on_device(activations, gain, shift, weight, cotangent):
    shape = activations.shape
    frames, rows, cols, chans = shape
    act, cot, taps = in_hbm(activations), in_hbm(cotangent), in_hbm(weight)
    parts = lax.axis_size("ta") * lax.axis_size("ha")
    gain, shift = gain.reshape(1, chans), shift.reshape(1, chans)
    gathered_shape = jax.ShapeDtypeStruct((parts, LANES), F32)
    edge = jax.ShapeDtypeStruct((2, frames, cols, chans), BF16)
    longer_shape = (frames, rows + 2, cols, chans)
    positions = frames * rows * cols

    pay, up, down = pl.pallas_call(
        stats_kernel,
        in_specs=[HBM, HBM],
        out_specs=[WHOLE] * 3,
        out_shape=[gathered_shape, edge, edge],
        scratch_shapes=[pltpu.VMEM(shape, BF16), DMA, DMA((4,))],
        compiler_params=params(16),
    )(act, cot)
    above = moved(up, 0, 1)
    below = moved(down, 0, -1)
    gathered = lax.all_to_all(pay, BOTH, 0, 0, tiled=True)

    def grad_scratch():
        return [
            pltpu.VMEM(longer_shape, BF16),
            pltpu.VMEM((6, 3, chans, chans), BF16),
            pltpu.VMEM((3, positions, chans), F32),
            DMA((3,)),
            DMA((6,)),
        ]

    early, longer = pl.pallas_call(
        lambda *refs: grad_kernel(0, 1, 0, 1, True, *refs),
        in_specs=[HBM] * 5,
        out_specs=[WHOLE] * 2,
        out_shape=[jax.ShapeDtypeStruct(shape, BF16), jax.ShapeDtypeStruct(longer_shape, BF16)],
        scratch_shapes=grad_scratch() + [DMA((3,))],
        compiler_params=params(32),
    )(cot, above, below, taps, act)
    early, longer, gathered = lax.optimization_barrier((early, longer, gathered))
    incoming = moved(early, -1, 0)
    prior = moved(longer, 1, 0)
    own = pl.pallas_call(
        lambda *refs: grad_kernel(2, 1, 1, 0, False, *refs),
        in_specs=[HBM] * 4,
        out_specs=WHOLE,
        out_shape=jax.ShapeDtypeStruct(shape, F32),
        scratch_shapes=grad_scratch(),
        compiler_params=params(32),
    )(cot, above, below, taps)
    pre_grad, pay, stats = pl.pallas_call(
        point_kernel,
        in_specs=[WHOLE] * 7,
        out_specs=[WHOLE] * 3,
        out_shape=[
            jax.ShapeDtypeStruct(shape, F32),
            gathered_shape,
            jax.ShapeDtypeStruct((2, 8, chans), F32),
        ],
        compiler_params=params(32),
    )(own, incoming, early, activations, gathered, gain, shift)
    gathered = lax.all_to_all(pay, BOTH, 0, 0, tiled=True)
    output = pl.pallas_call(
        conv_kernel,
        in_specs=[HBM] * 5 + [WHOLE] * 3,
        out_specs=WHOLE,
        out_shape=jax.ShapeDtypeStruct(shape, BF16),
        scratch_shapes=[
            pltpu.VMEM((frames + 2, rows + 2, cols, chans), BF16),
            pltpu.VMEM((frames + 2, rows + 2, cols, chans), BF16),
            pltpu.VMEM((9, 3, chans, chans), BF16),
            pltpu.VMEM((3, positions, chans), F32),
            DMA((4,)),
            DMA((9,)),
        ],
        compiler_params=params(44),
    )(act, above, below, prior, taps, stats, gain, shift)
    output, gathered = lax.optimization_barrier((output, gathered))
    input_grad = pl.pallas_call(
        final_kernel,
        in_specs=[WHOLE] * 5,
        out_specs=WHOLE,
        out_shape=jax.ShapeDtypeStruct(shape, BF16),
        compiler_params=params(32),
    )(pre_grad, activations, gathered, stats, gain)
    return (output, input_grad)


def solution(mesh):
    placed = (P("ta", "ha", None, None), P(), P(), P(), P("ta", "ha", None, None))
    return jax.shard_map(
        on_device,
        mesh=mesh,
        in_specs=placed,
        out_specs=(P("ta", "ha", None, None), P("ta", "ha", None, None)),
        check_vma=False,
    )
```

```python
import jax
import jax.numpy as jnp
from jax import lax
from jax.experimental import pallas as pl
from jax.experimental.pallas import tpu as pltpu
from jax.sharding import PartitionSpec as P

GROUPS = 32
LANES = 128
F32 = jnp.float32
BF16 = jnp.bfloat16
HBM = pl.BlockSpec(memory_space=pltpu.HBM)
ANY = pl.BlockSpec(memory_space=pl.ANY)
WHOLE = pl.BlockSpec(memory_space=pltpu.VMEM)
DMA = pltpu.SemaphoreType.DMA
BOTH = ("ta", "ha")


def params(mebibytes):
    return pltpu.CompilerParams(vmem_limit_bytes=mebibytes * 2**20)


def member(chans, offset, across):
    shape, chan_dim = ((LANES, chans), 1) if across else ((chans, LANES), 0)
    per_group = chans // GROUPS
    chan = lax.broadcasted_iota(jnp.int32, shape, chan_dim)
    lane = lax.broadcasted_iota(jnp.int32, shape, 1 - chan_dim) - offset
    inside = (chan >= lane * per_group) & (chan < (lane + 1) * per_group)
    return jnp.where(inside & (lane >= 0) & (lane < GROUPS), 1.0, 0.0).astype(F32)


def exact_dot(left, right):
    return jnp.dot(left, right, precision=lax.Precision.HIGHEST, preferred_element_type=F32)


def to_groups(by_chan, offset):
    lanes = exact_dot(by_chan, member(by_chan.shape[1], offset, False))
    return jnp.sum(lanes, axis=0, keepdims=True)


def to_chans(by_group, chans, offset):
    rows = jnp.broadcast_to(by_group, (8, LANES))
    return exact_dot(rows, member(chans, offset, True))


def eights(value):
    return value.reshape(value.shape[0] // 8, 8, value.shape[1])


def stats_kernel(act, cot, pay, up, down, block, load_sem, pack_sem):
    frames, rows, cols, chans = block.shape
    load = pltpu.make_async_copy(act, block, load_sem)
    load.start()
    packs = []
    for i, source in enumerate((act, cot)):
        packs.append(pltpu.make_async_copy(source.at[:, rows - 1], up.at[i], pack_sem.at[2 * i]))
        packs.append(pltpu.make_async_copy(source.at[:, 0], down.at[i], pack_sem.at[2 * i + 1]))
    for pack in packs:
        pack.start()
    load.wait()
    entries = frames * rows * cols * (chans // GROUPS)
    total = jnp.zeros((8, chans), F32)
    for t in range(frames):
        for h in range(rows):
            total = total + jnp.sum(eights(block[t, h].astype(F32)), axis=0)
    sums = to_groups(total, 0)
    mean = to_chans(sums / entries, chans, 0)
    spread = jnp.zeros((8, chans), F32)
    for t in range(frames):
        for h in range(rows):
            centered = eights(block[t, h].astype(F32)) - mean[None]
            spread = spread + jnp.sum(centered * centered, axis=0)
    row = sums + to_groups(spread, GROUPS)
    pay[...] = jnp.broadcast_to(row, pay.shape)
    for pack in packs:
        pack.wait()


def centre_kernel(cot, weight, taps, early, own, block, acc, late, load_sem, tap_sem, late_sem):
    rows, cols, chans = cot.shape[1:]
    half = rows * cols
    load = pltpu.make_async_copy(cot, block, load_sem)
    load.start()
    order = [(2, 1), (1, 1), (0, 1), (0, 0), (0, 2), (1, 0), (1, 2)]
    fetches = [pltpu.make_async_copy(weight.at[a, b], taps.at[a, b], tap_sem.at[a, b]) for a, b in order]
    fetches[0].start()
    fetches[1].start()
    load.wait()
    left = block[...].reshape(2 * half, chans)
    for n, a in enumerate((2, 1, 0)):
        fetches[n].wait()
        for fetch in (fetches[2:4], fetches[4:6], [])[n]:
            fetch.start()
        for c in range(3):
            term = transposed_dot(left, taps[a, 1, c])
            if a == 2:
                acc[1, c] = term
            elif a == 1:
                acc[1, c, :half] += term[half:]
                acc[0, c, half:] = term[:half]
            else:
                acc[0, c, :half] = term[:half]
                acc[0, c, half:] += term[half:]
        if a == 1:
            for fetch in fetches[6:]:
                fetch.start()
            combine(acc.at[1], late, 2, 0, None)
            send = pltpu.make_async_copy(late, own, late_sem)
            send.start()
    combine(acc.at[0], early, 2, 0, None)
    send.wait()
    for fetch in fetches[3:]:
        fetch.wait()


def transposed_dot(left, right):
    return lax.dot_general(left, right, (((1,), (1,)), ((), ())), preferred_element_type=F32)


def grad_products(full, part, source, target, ext, taps, acc, fetches=None):
    rows, cols, chans = ext.shape[1] - 2, ext.shape[2], ext.shape[3]
    half = rows * cols
    for b in (0, 2):
        both = ext[:, 2 - b : 2 - b + rows].reshape(2 * half, chans)
        one = ext[source, 2 - b : 2 - b + rows].reshape(half, chans)
        if fetches:
            fetches.pop(0).wait()
            fetches.pop(0).wait()
            for fetch in fetches:
                fetch.start()
        for c in range(3):
            term = transposed_dot(both, taps[full, b, c])
            if b == 0:
                acc[c] = term
            else:
                acc[c] += term
            acc[c, target * half : (target + 1) * half] += transposed_dot(one, taps[part, b, c])


def halo_copies(cot, above, below, ext, sem):
    rows = cot.shape[1]
    return [
        pltpu.make_async_copy(cot, ext.at[:, 1 : rows + 1], sem.at[0]),
        pltpu.make_async_copy(above.at[1], ext.at[:, 0], sem.at[1]),
        pltpu.make_async_copy(below.at[1], ext.at[:, rows + 1], sem.at[2]),
    ]


def early_kernel(cot, above, below, taps, centre, out, ext, acc, ext_sem):
    loads = halo_copies(cot, above, below, ext, ext_sem)
    for load in loads:
        load.start()
    for load in loads:
        load.wait()
    grad_products(0, 1, 0, 1, ext, taps, acc)
    combine(acc, out, 2, 0, centre)


def own_kernel(cot, above, below, weight, centre, act, gathered, gain, shift, out, longer, stats, ext, taps, acc, more, raw, acts, tap_sem, ext_sem, more_sem, raw_sem, acts_sem):
    frames, rows, cols, chans = act.shape
    load_act = pltpu.make_async_copy(act, raw, raw_sem)
    load_act.start()
    loads = halo_copies(cot, above, below, ext, ext_sem)
    loads.append(pltpu.make_async_copy(centre, more, more_sem))
    for load in loads:
        load.start()
    fetches = [
        pltpu.make_async_copy(weight.at[a, b], taps.at[a - 1, b], tap_sem.at[a - 1, b])
        for b in (0, 2)
        for a in (2, 1)
    ]
    fetches[0].start()
    fetches[1].start()
    entries = frames * rows * cols * (chans // GROUPS)
    mean, rstd = group_stats(gathered[...], entries, chans)
    stats[0] = mean
    stats[1] = rstd
    gains = jnp.broadcast_to(gain[...], (8, chans))
    shifts = jnp.broadcast_to(shift[...], (8, chans))
    row_at = lax.axis_index("ha")
    last_row = lax.axis_size("ha") - 1
    top = jnp.where(row_at == 0, 0.0, 1.0).astype(F32)
    bottom = jnp.where(row_at == last_row, 0.0, 1.0).astype(F32)

    def activate(values, t, i):
        normed = (eights(values.astype(F32)) - mean[None]) * rstd[None]
        pre = normed * gains[None] + shifts[None]
        value = pre / (1.0 + jnp.exp(-pre))
        if i == 0:
            value = value * top
        if i == rows + 1:
            value = value * bottom
        acts[t, i] = value.reshape(cols, chans).astype(BF16)

    for t in range(frames):
        activate(above[0, t], t, 0)
        activate(below[0, t], t, rows + 1)
    load_act.wait()
    sends = []
    for t in range(frames):
        for h in range(rows):
            activate(raw[t, h], t, 1 + h)
        sends.append(pltpu.make_async_copy(acts.at[t], longer.at[t], acts_sem.at[t]))
        sends[t].start()
    for load in loads:
        load.wait()
    grad_products(1, 0, 1, 0, ext, taps, acc, fetches)
    combine(acc, out, 2, 0, more)
    for send in sends:
        send.wait()


def combine(acc, out, earlier, later, more):
    frames, rows, cols, chans = out.shape
    col = lax.broadcasted_iota(jnp.int32, (cols, chans), 0)
    for t in range(frames):
        for h in range(rows):
            at = slice((t * rows + h) * cols, (t * rows + h + 1) * cols)
            before = jnp.where(col == 0, 0.0, pltpu.roll(acc[earlier, at], 1, 0))
            after = jnp.where(col == cols - 1, 0.0, pltpu.roll(acc[later, at], cols - 1, 0))
            total = before + acc[1, at] + after
            if more is not None:
                total = total + more[t, h]
            out[t, h] = total.astype(out.dtype)


def group_stats(gathered, entries, chans):
    parts = gathered.shape[0]
    count = parts * entries
    sums = jnp.sum(gathered, axis=0, keepdims=True)
    mean = sums / count
    apart = gathered * (1.0 / entries) - mean
    between = jnp.sum(apart * apart, axis=0, keepdims=True) * entries
    spread = to_chans(between, chans, 0) + to_chans(sums, chans, GROUPS)
    return to_chans(mean, chans, 0), lax.rsqrt(spread / count + 1e-06)


def point_kernel(own, incoming, early, act, stats, gain, shift, pre_grad, pay, block, block_sem):
    frames, rows, cols, chans = act.shape
    mean, rstd = stats[0], stats[1]
    first = lax.axis_index("ta") == 0
    scale = jnp.where(first, 1.0, 0.0).astype(F32)
    gains = jnp.broadcast_to(gain[...], (8, chans))
    shifts = jnp.broadcast_to(shift[...], (8, chans))
    shift_sum = jnp.zeros((8, chans), F32)
    gain_sum = jnp.zeros((8, chans), F32)
    sends = []
    for t in range(frames):
        for h in range(rows):
            grad = own[t, h] + incoming[t, h].astype(F32)
            if t == 0:
                grad = grad + scale * (early[0, h].astype(F32) + early[1, h].astype(F32))
            normed = (eights(act[t, h].astype(F32)) - mean[None]) * rstd[None]
            pre = normed * gains[None] + shifts[None]
            sig = 1.0 / (1.0 + jnp.exp(-pre))
            local = eights(grad) * sig * (1.0 + pre * (1.0 - sig))
            block[t, h] = local.reshape(cols, chans)
            shift_sum = shift_sum + jnp.sum(local, axis=0)
            gain_sum = gain_sum + jnp.sum(local * normed, axis=0)
            sends.append(pltpu.make_async_copy(block.at[t, h], pre_grad.at[t, h], block_sem.at[t, h]))
            sends[-1].start()
    row = to_groups(gains * shift_sum, 0) + to_groups(gains * gain_sum, GROUPS)
    pay[...] = jnp.broadcast_to(row, pay.shape)
    for send in sends:
        send.wait()


def conv_kernel(longer, prior, weight, out, ext, wide, taps, acc, ext_sem, tap_sem):
    frames, rows, cols, chans = out.shape
    first = lax.axis_index("ta") == 0
    own = pltpu.make_async_copy(longer, ext.at[frames:], ext_sem.at[0])
    own.start()

    @pl.when(first)
    def _():
        for t in range(frames):
            pltpu.make_async_copy(longer.at[0], ext.at[t], ext_sem.at[1 + t]).start()

    @pl.when(jnp.logical_not(first))
    def _():
        for t in range(frames):
            pltpu.make_async_copy(prior.at[t], ext.at[t], ext_sem.at[1 + t]).start()

    fetches = [pltpu.make_async_copy(weight.at[:, :, c], taps.at[c], tap_sem.at[c]) for c in range(3)]
    fetches[0].start()

    def widen(a):
        for b in range(3):
            k = (3 * a + b) * chans
            wide[:, :, :, k : k + chans] = ext[a : a + frames, b : b + rows]

    own.wait()
    widen(2)
    for t in range(frames):
        pltpu.make_async_copy(prior.at[t], ext.at[t], ext_sem.at[1 + t]).wait()
    widen(1)
    widen(0)
    left = wide[...].reshape(frames * rows * cols, 9 * chans)
    for c in range(3):
        fetches[c].wait()
        if c < 2:
            fetches[c + 1].start()
        acc[c] = jnp.dot(left, taps[c].reshape(9 * chans, chans), preferred_element_type=F32)
    combine(acc, out, 0, 2, None)


def final_kernel(pre_grad, act, gathered, stats, gain, out):
    frames, rows, cols, chans = act.shape
    count = gathered.shape[0] * frames * rows * cols * (chans // GROUPS)
    sums = jnp.sum(gathered[...], axis=0, keepdims=True) / count
    first = to_chans(sums, chans, 0)
    second = to_chans(sums, chans, GROUPS)
    mean, rstd = stats[0], stats[1]
    gains = jnp.broadcast_to(gain[...], (8, chans))
    for t in range(frames):
        for h in range(rows):
            normed = (eights(act[t, h].astype(F32)) - mean[None]) * rstd[None]
            value = rstd[None] * (eights(pre_grad[t, h]) * gains[None] - first[None] - normed * second[None])
            out[t, h] = value.reshape(cols, chans).astype(BF16)


def moved(value, frame_step, row_step):
    frames, rows = lax.axis_size("ta"), lax.axis_size("ha")
    pairs = []
    for t in range(frames):
        for h in range(rows):
            to_t, to_h = t + frame_step, h + row_step
            if 0 <= to_t < frames and 0 <= to_h < rows:
                pairs.append((t * rows + h, to_t * rows + to_h))
    return lax.ppermute(value, BOTH, pairs)


def in_hbm(value):
    return pltpu.with_memory_space_constraint(value, pltpu.HBM)


def in_vmem(value):
    return pltpu.with_memory_space_constraint(value, pltpu.VMEM)


def on_device(activations, gain, shift, weight, cotangent):
    shape = activations.shape
    frames, rows, cols, chans = shape
    act, cot, taps = in_hbm(activations), in_hbm(cotangent), in_hbm(weight)
    parts = lax.axis_size("ta") * lax.axis_size("ha")
    gain, shift = gain.reshape(1, chans), shift.reshape(1, chans)
    gathered_shape = jax.ShapeDtypeStruct((parts, LANES), F32)
    edge = jax.ShapeDtypeStruct((2, frames, cols, chans), BF16)
    longer_shape = (frames, rows + 2, cols, chans)
    positions = frames * rows * cols

    pay, up, down = pl.pallas_call(
        stats_kernel,
        in_specs=[HBM, HBM],
        out_specs=[WHOLE] * 3,
        out_shape=[gathered_shape, edge, edge],
        scratch_shapes=[pltpu.VMEM(shape, BF16), DMA, DMA((4,))],
        compiler_params=params(16),
    )(act, cot)
    above = moved(up, 0, 1)
    below = moved(down, 0, -1)
    gathered = lax.all_to_all(pay, BOTH, 0, 0, tiled=True)

    f32_block = jax.ShapeDtypeStruct(shape, F32)
    sums = (3, positions, chans)
    held, early_centre, own_centre = pl.pallas_call(
        centre_kernel,
        in_specs=[HBM] * 2,
        out_specs=[WHOLE, WHOLE, HBM],
        out_shape=[pltpu.VMEM(weight.shape, BF16), f32_block, pltpu.HBM(shape, F32)],
        scratch_shapes=[
            pltpu.VMEM(shape, BF16),
            pltpu.VMEM((2,) + sums, F32),
            pltpu.VMEM(shape, F32),
            DMA,
            DMA((3, 3)),
            DMA,
        ],
        compiler_params=params(16),
    )(cot, taps)
    held = in_vmem(held)
    early = pl.pallas_call(
        early_kernel,
        in_specs=[HBM, WHOLE, WHOLE, WHOLE, WHOLE],
        out_specs=WHOLE,
        out_shape=jax.ShapeDtypeStruct(shape, BF16),
        scratch_shapes=[pltpu.VMEM(longer_shape, BF16), pltpu.VMEM(sums, F32), DMA((3,))],
        compiler_params=params(12),
    )(cot, above, below, held, early_centre)
    early, gathered = lax.optimization_barrier((early, gathered))
    incoming = moved(early, -1, 0)
    own, longer, stats = pl.pallas_call(
        own_kernel,
        in_specs=[HBM, WHOLE, WHOLE, HBM, HBM, HBM, WHOLE, WHOLE, WHOLE],
        out_specs=[WHOLE, HBM, WHOLE],
        out_shape=[f32_block, pltpu.HBM(longer_shape, BF16), jax.ShapeDtypeStruct((2, 8, chans), F32)],
        scratch_shapes=[
            pltpu.VMEM(longer_shape, BF16),
            pltpu.VMEM((2, 3, 3, chans, chans), BF16),
            pltpu.VMEM(sums, F32),
            pltpu.VMEM(shape, F32),
            pltpu.VMEM(shape, BF16),
            pltpu.VMEM(longer_shape, BF16),
            DMA((2, 3)),
            DMA((3,)),
            DMA,
            DMA,
            DMA((frames,)),
        ],
        compiler_params=params(28),
    )(cot, above, below, taps, in_hbm(own_centre), act, gathered, gain, shift)
    longer, incoming = lax.optimization_barrier((longer, incoming))
    prior = moved(longer, 1, 0)
    pre_grad, pay = pl.pallas_call(
        point_kernel,
        in_specs=[WHOLE] * 7,
        out_specs=[HBM, WHOLE],
        out_shape=[pltpu.HBM(shape, F32), gathered_shape],
        scratch_shapes=[pltpu.VMEM(shape, F32), DMA((frames, rows))],
        compiler_params=params(16),
    )(own, incoming, early, activations, stats, gain, shift)
    gathered = lax.all_to_all(pay, BOTH, 0, 0, tiled=True)
    output = pl.pallas_call(
        conv_kernel,
        in_specs=[HBM, ANY, HBM],
        out_specs=WHOLE,
        out_shape=jax.ShapeDtypeStruct(shape, BF16),
        scratch_shapes=[
            pltpu.VMEM((frames + 2, rows + 2, cols, chans), BF16),
            pltpu.VMEM((frames, rows, cols, 9 * chans), BF16),
            pltpu.VMEM((3, 3, 3, chans, chans), BF16),
            pltpu.VMEM(sums, F32),
            DMA((1 + frames,)),
            DMA((3,)),
        ],
        compiler_params=params(36),
    )(in_hbm(longer), prior, taps)
    output, gathered = lax.optimization_barrier((output, gathered))
    input_grad = pl.pallas_call(
        final_kernel,
        in_specs=[WHOLE] * 5,
        out_specs=WHOLE,
        out_shape=jax.ShapeDtypeStruct(shape, BF16),
        compiler_params=params(16),
    )(pre_grad, activations, gathered, stats, gain)
    return (output, input_grad)


def solution(mesh):
    placed = (P("ta", "ha", None, None), P(), P(), P(), P("ta", "ha", None, None))
    return jax.shard_map(
        on_device,
        mesh=mesh,
        in_specs=placed,
        out_specs=(P("ta", "ha", None, None), P("ta", "ha", None, None)),
        check_vma=False,
    )
```

```python
import jax
import jax.numpy as jnp
from jax import lax
from jax.experimental import pallas as pl
from jax.experimental.pallas import tpu as pltpu
from jax.sharding import PartitionSpec as P

GROUPS = 32
LANES = 128
F32 = jnp.float32
BF16 = jnp.bfloat16
HBM = pl.BlockSpec(memory_space=pltpu.HBM)
ANY = pl.BlockSpec(memory_space=pl.ANY)
WHOLE = pl.BlockSpec(memory_space=pltpu.VMEM)
DMA = pltpu.SemaphoreType.DMA
BOTH = ("ta", "ha")


def params(mebibytes):
    return pltpu.CompilerParams(vmem_limit_bytes=mebibytes * 2**20)


def member(chans, across):
    shape, chan_dim = ((LANES, chans), 1) if across else ((chans, LANES), 0)
    per_group = chans // GROUPS
    chan = lax.broadcasted_iota(jnp.int32, shape, chan_dim)
    lane = lax.broadcasted_iota(jnp.int32, shape, 1 - chan_dim)
    inside = (chan >= lane * per_group) & (chan < (lane + 1) * per_group)
    return jnp.where(inside, 1.0, 0.0).astype(BF16)


def exact_dot(left, right):
    high = left.astype(BF16).astype(F32)
    rest = left - high
    middle = rest.astype(BF16).astype(F32)
    parts = jnp.concatenate([high, middle, rest - middle], axis=0).astype(BF16)
    out = jnp.dot(parts, right, preferred_element_type=F32)
    rows = left.shape[0]
    return out[2 * rows :] + out[rows : 2 * rows] + out[:rows]


def to_groups(one, two):
    lanes = exact_dot(jnp.concatenate([one, two], axis=0), member(one.shape[1], False))
    return jnp.sum(lanes[:8] + pltpu.roll(lanes[8:], GROUPS, 1), axis=0, keepdims=True)


def to_chans(one, two, chans):
    rows = jnp.concatenate([jnp.broadcast_to(one, (8, LANES)), jnp.broadcast_to(two, (8, LANES))], axis=0)
    out = exact_dot(rows, member(chans, True))
    return out[:8], out[8:]


def second_part(row):
    return pltpu.roll(jnp.broadcast_to(row, (8, LANES)), LANES - GROUPS, 1)[:1]


def eights(value):
    return value.reshape(value.shape[0] // 8, 8, value.shape[1])


def stats_kernel(act, cot, pay, up, down, act_sem, cot_sem):
    frames, rows, cols, chans = act.shape
    sides = ((0, down), (rows - 1, up))
    loads = []
    for t in range(frames):
        for n, (h, side) in enumerate(sides):
            loads.append(pltpu.make_async_copy(act.at[t, h], side.at[0, t], act_sem.at[t, n]))
            loads[-1].start()
    packs = [pltpu.make_async_copy(cot.at[:, h], side.at[1], cot_sem.at[n]) for n, (h, side) in enumerate(sides)]
    for pack in packs:
        pack.start()
    blocks = [(t, side) for t in range(frames) for _, side in sides]
    entries = frames * rows * cols * (chans // GROUPS)
    none = jnp.zeros((8, chans), F32)
    total = none
    for load, (t, side) in zip(loads, blocks):
        load.wait()
        total = total + jnp.sum(eights(side[0, t].astype(F32)), axis=0)
    sums = to_groups(total, none)
    mean, _ = to_chans(sums / entries, sums, chans)
    spread = none
    for t, side in blocks:
        centered = eights(side[0, t].astype(F32)) - mean[None]
        spread = spread + jnp.sum(centered * centered, axis=0)
    row = sums + to_groups(none, spread)
    pay[...] = jnp.broadcast_to(row, pay.shape)
    for pack in packs:
        pack.wait()


def centre_kernel(cot, weight, taps, early, own, block, acc, late, load_sem, tap_sem, late_sem):
    rows, cols, chans = cot.shape[1:]
    half = rows * cols
    load = pltpu.make_async_copy(cot, block, load_sem)
    load.start()
    order = [(2, 1), (1, 1), (0, 1), (0, 0), (0, 2), (1, 0), (1, 2)]
    fetches = [pltpu.make_async_copy(weight.at[a, b], taps.at[a, b], tap_sem.at[a, b]) for a, b in order]
    fetches[0].start()
    fetches[1].start()
    load.wait()
    left = block[...].reshape(2 * half, chans)
    for n, a in enumerate((2, 1, 0)):
        fetches[n].wait()
        for fetch in (fetches[2:4], fetches[4:6], [])[n]:
            fetch.start()
        for c in range(3):
            term = transposed_dot(left, taps[a, 1, c])
            if a == 2:
                acc[1, c] = term
            elif a == 1:
                acc[1, c, :half] += term[half:]
                acc[0, c, half:] = term[:half]
            else:
                acc[0, c, :half] = term[:half]
                acc[0, c, half:] += term[half:]
        if a == 1:
            for fetch in fetches[6:]:
                fetch.start()
            combine(acc.at[1], late, 2, 0, None)
            send = pltpu.make_async_copy(late, own, late_sem)
            send.start()
    combine(acc.at[0], early, 2, 0, None)
    send.wait()
    for fetch in fetches[3:]:
        fetch.wait()


def transposed_dot(left, right):
    return lax.dot_general(left, right, (((1,), (1,)), ((), ())), preferred_element_type=F32)


def grad_products(full, part, source, target, lefts, taps, acc, before=None):
    half = lefts[0].shape[1] * lefts[0].shape[2]
    chans = lefts[0].shape[3]
    for n, b in enumerate((0, 2)):
        if before is not None:
            before(n)
        both = lefts[n][...].reshape(2 * half, chans)
        one = lefts[n][source].reshape(half, chans)
        for c in range(3):
            term = transposed_dot(both, taps[full, b, c])
            if b == 0:
                acc[c] = term
            else:
                acc[c] += term
            acc[c, target * half : (target + 1) * half] += transposed_dot(one, taps[part, b, c])


def fill_lefts(cot, above, below, lefts):
    for t in range(cot.shape[0]):
        lefts[0, t, 0] = cot[t, 1]
        lefts[0, t, 1] = below[1, t]
        lefts[1, t, 0] = above[1, t]
        lefts[1, t, 1] = cot[t, 0]


def early_kernel(cot, above, below, taps, centre, out, lefts, acc):
    fill_lefts(cot, above, below, lefts)
    grad_products(0, 1, 0, 1, (lefts.at[0], lefts.at[1]), taps, acc)
    combine(acc, out, 2, 0, centre)


def own_kernel(cot, above, below, weight, centre, act, gathered, gain, shift, out, longer, stats, lefts, taps, acc, more, raw, block, acts, tap_sem, more_sem, raw_sem, block_sem, acts_sem):
    frames, rows, cols, chans = act.shape
    load_act = pltpu.make_async_copy(act, raw, raw_sem)
    load_act.start()
    load_cot = pltpu.make_async_copy(cot, block, block_sem)
    load_cot.start()
    fetches = [
        [pltpu.make_async_copy(weight.at[a, b], taps.at[a - 1, b], tap_sem.at[a - 1, b]) for a in (2, 1)]
        for b in (0, 2)
    ]
    for fetch in fetches[0]:
        fetch.start()
    load_more = pltpu.make_async_copy(centre, more, more_sem)
    entries = frames * rows * cols * (chans // GROUPS)
    mean, rstd = group_stats(gathered[...], entries, chans)
    stats[0] = mean
    stats[1] = rstd
    gains = jnp.broadcast_to(gain[...], (8, chans))
    shifts = jnp.broadcast_to(shift[...], (8, chans))
    row_at = lax.axis_index("ha")
    last_row = lax.axis_size("ha") - 1
    top = jnp.where(row_at == 0, 0.0, 1.0).astype(F32)
    bottom = jnp.where(row_at == last_row, 0.0, 1.0).astype(F32)

    def activate(values, t, i):
        normed = (eights(values.astype(F32)) - mean[None]) * rstd[None]
        pre = normed * gains[None] + shifts[None]
        value = pre / (1.0 + jnp.exp(-pre))
        if i == 0:
            value = value * top
        if i == rows + 1:
            value = value * bottom
        acts[t, i] = value.reshape(cols, chans).astype(BF16)

    for t in range(frames):
        activate(above[0, t], t, 0)
        activate(below[0, t], t, rows + 1)
    load_act.wait()
    sends = []
    for t in range(frames):
        for h in range(rows):
            activate(raw[t, h], t, 1 + h)
        sends.append(pltpu.make_async_copy(acts.at[t], longer.at[t], acts_sem.at[t]))
        sends[t].start()
    load_cot.wait()
    fill_lefts(block, above, below, lefts)

    def before(n):
        for fetch in fetches[n]:
            fetch.wait()
        if n == 0:
            for fetch in fetches[1]:
                fetch.start()
            load_more.start()

    grad_products(1, 0, 1, 0, (lefts.at[0], lefts.at[1]), taps, acc, before)
    load_more.wait()
    combine(acc, out, 2, 0, more)
    for send in sends:
        send.wait()


def combine(acc, out, earlier, later, more):
    frames, rows, cols, chans = out.shape
    col = lax.broadcasted_iota(jnp.int32, (cols, chans), 0)
    for t in range(frames):
        for h in range(rows):
            at = slice((t * rows + h) * cols, (t * rows + h + 1) * cols)
            before = jnp.where(col == 0, 0.0, pltpu.roll(acc[earlier, at], 1, 0))
            after = jnp.where(col == cols - 1, 0.0, pltpu.roll(acc[later, at], cols - 1, 0))
            total = before + acc[1, at] + after
            if more is not None:
                total = total + more[t, h]
            out[t, h] = total.astype(out.dtype)


def group_stats(gathered, entries, chans):
    parts = gathered.shape[0]
    count = parts * entries
    sums = jnp.sum(gathered, axis=0, keepdims=True)
    mean = sums / count
    apart = gathered * (1.0 / entries) - mean
    between = jnp.sum(apart * apart, axis=0, keepdims=True) * entries
    var = (between + second_part(sums)) / count
    lane = lax.broadcasted_iota(jnp.int32, (1, LANES), 1)
    rstd = jnp.where(lane < GROUPS, lax.rsqrt(jnp.where(lane < GROUPS, var, 1.0) + 1e-06), 0.0)
    return to_chans(mean, rstd, chans)


def point_kernel(own, incoming, early, act, stats, gain, shift, pre_grad, pay, block, block_sem):
    frames, rows, cols, chans = act.shape
    mean, rstd = stats[0], stats[1]
    first = lax.axis_index("ta") == 0
    scale = jnp.where(first, 1.0, 0.0).astype(F32)
    gains = jnp.broadcast_to(gain[...], (8, chans))
    shifts = jnp.broadcast_to(shift[...], (8, chans))
    shift_sum = jnp.zeros((8, chans), F32)
    gain_sum = jnp.zeros((8, chans), F32)
    sends = []
    for t in range(frames):
        for h in range(rows):
            grad = own[t, h] + incoming[t, h].astype(F32)
            if t == 0:
                grad = grad + scale * (early[0, h].astype(F32) + early[1, h].astype(F32))
            normed = (eights(act[t, h].astype(F32)) - mean[None]) * rstd[None]
            pre = normed * gains[None] + shifts[None]
            sig = 1.0 / (1.0 + jnp.exp(-pre))
            local = eights(grad) * sig * (1.0 + pre * (1.0 - sig))
            block[t, h] = local.reshape(cols, chans)
            shift_sum = shift_sum + jnp.sum(local, axis=0)
            gain_sum = gain_sum + jnp.sum(local * normed, axis=0)
            sends.append(pltpu.make_async_copy(block.at[t, h], pre_grad.at[t, h], block_sem.at[t, h]))
            sends[-1].start()
    row = to_groups(gains * shift_sum, gains * gain_sum)
    pay[...] = jnp.broadcast_to(row, pay.shape)
    for send in sends:
        send.wait()


def conv_kernel(longer, prior, weight, out, ext, near, far, near_taps, far_taps, acc, ext_sem, near_sem, far_sem):
    frames, rows, cols, chans = out.shape
    positions = frames * rows * cols
    first = lax.axis_index("ta") == 0
    own = pltpu.make_async_copy(longer, ext.at[frames:], ext_sem.at[0])
    own.start()
    fetches = [pltpu.make_async_copy(weight.at[2, :, c], near_taps.at[c], near_sem.at[c]) for c in range(3)]
    fetches += [pltpu.make_async_copy(weight.at[0:2, :, c], far_taps.at[c], far_sem.at[c]) for c in range(3)]
    fetches[0].start()

    @pl.when(first)
    def _():
        for t in range(frames):
            pltpu.make_async_copy(longer.at[0], ext.at[t], ext_sem.at[1 + t]).start()

    @pl.when(jnp.logical_not(first))
    def _():
        for t in range(frames):
            pltpu.make_async_copy(prior.at[t], ext.at[t], ext_sem.at[1 + t]).start()

    fetches[1].start()
    own.wait()
    for b in range(3):
        near[:, :, :, b * chans : (b + 1) * chans] = ext[2 : 2 + frames, b : b + rows]
    left = near[...].reshape(positions, 3 * chans)
    for c in range(3):
        fetches[c].wait()
        fetches[c + 2].start()
        acc[c] = jnp.dot(left, near_taps[c].reshape(3 * chans, chans), preferred_element_type=F32)
    for t in range(frames):
        pltpu.make_async_copy(prior.at[t], ext.at[t], ext_sem.at[1 + t]).wait()
    for a in range(2):
        for b in range(3):
            k = (3 * a + b) * chans
            far[:, :, :, k : k + chans] = ext[a : a + frames, b : b + rows]
    left = far[...].reshape(positions, 6 * chans)
    for c in range(3):
        fetches[3 + c].wait()
        if c == 0:
            fetches[5].start()
        acc[c] += jnp.dot(left, far_taps[c].reshape(6 * chans, chans), preferred_element_type=F32)
    combine(acc, out, 0, 2, None)


def final_kernel(pre_grad, act, gathered, stats, gain, out):
    frames, rows, cols, chans = act.shape
    count = gathered.shape[0] * frames * rows * cols * (chans // GROUPS)
    sums = jnp.sum(gathered[...], axis=0, keepdims=True) / count
    first, second = to_chans(sums, second_part(sums), chans)
    mean, rstd = stats[0], stats[1]
    gains = jnp.broadcast_to(gain[...], (8, chans))
    for t in range(frames):
        for h in range(rows):
            normed = (eights(act[t, h].astype(F32)) - mean[None]) * rstd[None]
            value = rstd[None] * (eights(pre_grad[t, h]) * gains[None] - first[None] - normed * second[None])
            out[t, h] = value.reshape(cols, chans).astype(BF16)


def moved(value, frame_step, row_step):
    frames, rows = lax.axis_size("ta"), lax.axis_size("ha")
    pairs = []
    for t in range(frames):
        for h in range(rows):
            to_t, to_h = t + frame_step, h + row_step
            if 0 <= to_t < frames and 0 <= to_h < rows:
                pairs.append((t * rows + h, to_t * rows + to_h))
    return lax.ppermute(value, BOTH, pairs)


def in_hbm(value):
    return pltpu.with_memory_space_constraint(value, pltpu.HBM)


def in_vmem(value):
    return pltpu.with_memory_space_constraint(value, pltpu.VMEM)


def on_device(activations, gain, shift, weight, cotangent):
    shape = activations.shape
    frames, rows, cols, chans = shape
    act, cot, taps = in_hbm(activations), in_hbm(cotangent), in_hbm(weight)
    parts = lax.axis_size("ta") * lax.axis_size("ha")
    gain, shift = gain.reshape(1, chans), shift.reshape(1, chans)
    gathered_shape = jax.ShapeDtypeStruct((parts, LANES), F32)
    edge = jax.ShapeDtypeStruct((2, frames, cols, chans), BF16)
    longer_shape = (frames, rows + 2, cols, chans)
    positions = frames * rows * cols

    pay, up, down = pl.pallas_call(
        stats_kernel,
        in_specs=[HBM, HBM],
        out_specs=[WHOLE] * 3,
        out_shape=[gathered_shape, edge, edge],
        scratch_shapes=[DMA((frames, rows)), DMA((2,))],
        compiler_params=params(16),
    )(act, cot)
    above = moved(up, 0, 1)
    below = moved(down, 0, -1)
    gathered = lax.all_to_all(pay, BOTH, 0, 0, tiled=True)

    f32_block = jax.ShapeDtypeStruct(shape, F32)
    sums = (3, positions, chans)
    held, early_centre, own_centre, cot_held = pl.pallas_call(
        centre_kernel,
        in_specs=[HBM] * 2,
        out_specs=[WHOLE, WHOLE, HBM, WHOLE],
        out_shape=[pltpu.VMEM(weight.shape, BF16), f32_block, pltpu.HBM(shape, F32), jax.ShapeDtypeStruct(shape, BF16)],
        scratch_shapes=[
            pltpu.VMEM((2,) + sums, F32),
            pltpu.VMEM(shape, F32),
            DMA,
            DMA((3, 3)),
            DMA,
        ],
        compiler_params=params(16),
    )(cot, taps)
    held = in_vmem(held)
    early = pl.pallas_call(
        early_kernel,
        in_specs=[WHOLE] * 5,
        out_specs=WHOLE,
        out_shape=jax.ShapeDtypeStruct(shape, BF16),
        scratch_shapes=[pltpu.VMEM((2,) + shape, BF16), pltpu.VMEM(sums, F32)],
        compiler_params=params(16),
    )(cot_held, above, below, held, early_centre)
    early, gathered = lax.optimization_barrier((early, gathered))
    incoming = moved(early, -1, 0)
    own, longer, stats = pl.pallas_call(
        own_kernel,
        in_specs=[HBM, WHOLE, WHOLE, HBM, HBM, HBM, WHOLE, WHOLE, WHOLE],
        out_specs=[WHOLE, HBM, WHOLE],
        out_shape=[f32_block, pltpu.HBM(longer_shape, BF16), jax.ShapeDtypeStruct((2, 8, chans), F32)],
        scratch_shapes=[
            pltpu.VMEM((2,) + shape, BF16),
            pltpu.VMEM((2, 3, 3, chans, chans), BF16),
            pltpu.VMEM(sums, F32),
            pltpu.VMEM(shape, F32),
            pltpu.VMEM(shape, BF16),
            pltpu.VMEM(shape, BF16),
            pltpu.VMEM(longer_shape, BF16),
            DMA((2, 3)),
            DMA,
            DMA,
            DMA,
            DMA((frames,)),
        ],
        compiler_params=params(28),
    )(cot, above, below, taps, in_hbm(own_centre), act, gathered, gain, shift)
    longer, incoming = lax.optimization_barrier((longer, incoming))
    prior = moved(longer, 1, 0)
    pre_grad, pay = pl.pallas_call(
        point_kernel,
        in_specs=[WHOLE] * 7,
        out_specs=[HBM, WHOLE],
        out_shape=[pltpu.HBM(shape, F32), gathered_shape],
        scratch_shapes=[pltpu.VMEM(shape, F32), DMA((frames, rows))],
        compiler_params=params(16),
    )(own, incoming, early, activations, stats, gain, shift)
    gathered = lax.all_to_all(pay, BOTH, 0, 0, tiled=True)
    output = pl.pallas_call(
        conv_kernel,
        in_specs=[HBM, ANY, HBM],
        out_specs=WHOLE,
        out_shape=jax.ShapeDtypeStruct(shape, BF16),
        scratch_shapes=[
            pltpu.VMEM((frames + 2, rows + 2, cols, chans), BF16),
            pltpu.VMEM((frames, rows, cols, 3 * chans), BF16),
            pltpu.VMEM((frames, rows, cols, 6 * chans), BF16),
            pltpu.VMEM((3, 3, chans, chans), BF16),
            pltpu.VMEM((3, 2, 3, chans, chans), BF16),
            pltpu.VMEM(sums, F32),
            DMA((1 + frames,)),
            DMA((3,)),
            DMA((3,)),
        ],
        compiler_params=params(36),
    )(in_hbm(longer), prior, taps)
    output, gathered = lax.optimization_barrier((output, gathered))
    input_grad = pl.pallas_call(
        final_kernel,
        in_specs=[WHOLE] * 5,
        out_specs=WHOLE,
        out_shape=jax.ShapeDtypeStruct(shape, BF16),
        compiler_params=params(16),
    )(pre_grad, activations, gathered, stats, gain)
    return (output, input_grad)


def solution(mesh):
    placed = (P("ta", "ha", None, None), P(), P(), P(), P("ta", "ha", None, None))
    return jax.shard_map(
        on_device,
        mesh=mesh,
        in_specs=placed,
        out_specs=(P("ta", "ha", None, None), P("ta", "ha", None, None)),
        check_vma=False,
    )
```

```python
import jax
import jax.numpy as jnp
from jax import lax
from jax.experimental import pallas as pl
from jax.experimental.pallas import tpu as pltpu
from jax.sharding import PartitionSpec as P

GROUPS = 32
LANES = 128
F32 = jnp.float32
BF16 = jnp.bfloat16
HBM = pl.BlockSpec(memory_space=pltpu.HBM)
ANY = pl.BlockSpec(memory_space=pl.ANY)
WHOLE = pl.BlockSpec(memory_space=pltpu.VMEM)
DMA = pltpu.SemaphoreType.DMA
BOTH = ("ta", "ha")


def params(mebibytes):
    return pltpu.CompilerParams(vmem_limit_bytes=mebibytes * 2**20)


def member(chans, across):
    shape, chan_dim = ((LANES, chans), 1) if across else ((chans, LANES), 0)
    per_group = chans // GROUPS
    chan = lax.broadcasted_iota(jnp.int32, shape, chan_dim)
    lane = lax.broadcasted_iota(jnp.int32, shape, 1 - chan_dim)
    inside = (chan >= lane * per_group) & (chan < (lane + 1) * per_group)
    return jnp.where(inside, 1.0, 0.0).astype(BF16)


def exact_dot(left, right):
    high = left.astype(BF16).astype(F32)
    rest = left - high
    middle = rest.astype(BF16).astype(F32)
    parts = jnp.concatenate([high, middle, rest - middle], axis=0).astype(BF16)
    out = jnp.dot(parts, right, preferred_element_type=F32)
    rows = left.shape[0]
    return out[2 * rows :] + out[rows : 2 * rows] + out[:rows]


def to_groups(one, two):
    lanes = exact_dot(jnp.concatenate([one, two], axis=0), member(one.shape[1], False))
    return jnp.sum(lanes[:8] + pltpu.roll(lanes[8:], GROUPS, 1), axis=0, keepdims=True)


def to_chans(one, two, chans):
    rows = jnp.concatenate([jnp.broadcast_to(one, (8, LANES)), jnp.broadcast_to(two, (8, LANES))], axis=0)
    out = exact_dot(rows, member(chans, True))
    return out[:8], out[8:]


def second_part(row):
    return pltpu.roll(jnp.broadcast_to(row, (8, LANES)), LANES - GROUPS, 1)[:1]


def eights(value):
    return value.reshape(value.shape[0] // 8, 8, value.shape[1])


def stats_kernel(act, cot, pay, up, down, act_sem, cot_sem):
    frames, rows, cols, chans = act.shape
    sides = ((0, down), (rows - 1, up))
    loads = []
    for t in range(frames):
        for n, (h, side) in enumerate(sides):
            loads.append(pltpu.make_async_copy(act.at[t, h], side.at[0, t], act_sem.at[t, n]))
            loads[-1].start()
    packs = [pltpu.make_async_copy(cot.at[:, h], side.at[1], cot_sem.at[n]) for n, (h, side) in enumerate(sides)]
    for pack in packs:
        pack.start()
    blocks = [(t, side) for t in range(frames) for _, side in sides]
    entries = frames * rows * cols * (chans // GROUPS)
    none = jnp.zeros((8, chans), F32)
    total = none
    for load, (t, side) in zip(loads, blocks):
        load.wait()
        total = total + jnp.sum(eights(side[0, t].astype(F32)), axis=0)
    sums = to_groups(total, none)
    mean, _ = to_chans(sums / entries, sums, chans)
    spread = none
    for t, side in blocks:
        centered = eights(side[0, t].astype(F32)) - mean[None]
        spread = spread + jnp.sum(centered * centered, axis=0)
    row = sums + to_groups(none, spread)
    pay[...] = jnp.broadcast_to(row, pay.shape)
    for pack in packs:
        pack.wait()


def centre_kernel(up, down, weight, taps, early, own, block, acc, late, tap_sem, late_sem):
    frames, cols, chans = up.shape[1:]
    rows = 2
    half = rows * cols
    order = [(2, 1), (1, 1), (0, 1), (0, 0), (0, 2), (1, 0), (1, 2)]
    fetches = [pltpu.make_async_copy(weight.at[a, b], taps.at[a, b], tap_sem.at[a, b]) for a, b in order]
    fetches[0].start()
    fetches[1].start()
    for t in range(frames):
        block[t, 0] = down[1, t]
        block[t, 1] = up[1, t]
    left = block[...].reshape(2 * half, chans)
    for n, a in enumerate((2, 1, 0)):
        fetches[n].wait()
        for fetch in (fetches[2:4], fetches[4:6], [])[n]:
            fetch.start()
        for c in (0, 2, 1):
            if a < 2 and c == 1:
                sides(acc.at[a], 2, 0, 2 * rows)
            term = transposed_dot(left, taps[a, 1, c])
            if a == 2:
                acc[1, c] = term
            elif a == 1:
                acc[1, c, :half] += term[half:]
                acc[0, c, half:] = term[:half]
            else:
                acc[0, c, :half] = term[:half]
                acc[0, c, half:] += term[half:]
        if a == 1:
            for fetch in fetches[6:]:
                fetch.start()
            finish(acc.at[1], late, 2, None)
            send = pltpu.make_async_copy(late, own, late_sem)
            send.start()
    finish(acc.at[0], early, 2, None)
    send.wait()
    for fetch in fetches[3:]:
        fetch.wait()


def transposed_dot(left, right):
    return lax.dot_general(left, right, (((1,), (1,)), ((), ())), preferred_element_type=F32)


def grad_products(full, part, source, target, lefts, taps, acc, before=None, between=None):
    half = lefts[0].shape[1] * lefts[0].shape[2]
    chans = lefts[0].shape[3]
    for n, b in enumerate((0, 2)):
        if before is not None:
            before(n)
        both = lefts[n][...].reshape(2 * half, chans)
        one = lefts[n][source].reshape(half, chans)
        for c in (0, 2, 1):
            if b == 2 and c == 1:
                sides(acc, 2, 0, half // lefts[0].shape[2] * 2)
            term = transposed_dot(both, taps[full, b, c])
            if b == 0:
                acc[c] = term
            else:
                acc[c] += term
            if between is not None:
                between(b, c)
            acc[c, target * half : (target + 1) * half] += transposed_dot(one, taps[part, b, c])


def fill_lefts(cot, above, below, lefts):
    for t in range(lefts.shape[1]):
        lefts[0, t, 0] = cot[1][1, t]
        lefts[0, t, 1] = below[1, t]
        lefts[1, t, 0] = above[1, t]
        lefts[1, t, 1] = cot[0][1, t]


def early_kernel(up, down, above, below, taps, centre, out, longer, lefts, acc, send_sem):
    sends = [
        pltpu.make_async_copy(side.at[0, t], longer.at[t, n], send_sem.at[t, n])
        for n, side in enumerate((above, down, up, below))
        for t in range(out.shape[0])
    ]
    for send in sends:
        send.start()
    fill_lefts((down, up), above, below, lefts)
    grad_products(0, 1, 0, 1, (lefts.at[0], lefts.at[1]), taps, acc)
    finish(acc, out, 2, centre)
    for send in sends:
        send.wait()


def activation(mean, rstd, gain, shift, out):
    chans, rows = out.shape[3], out.shape[1]
    gains = jnp.broadcast_to(gain[...], (8, chans))
    shifts = jnp.broadcast_to(shift[...], (8, chans))
    row_at = lax.axis_index("ha")
    last_row = lax.axis_size("ha") - 1
    top = jnp.where(row_at == 0, 0.0, 1.0).astype(F32)
    bottom = jnp.where(row_at == last_row, 0.0, 1.0).astype(F32)

    def activate(values, t, i):
        normed = (eights(values.astype(F32)) - mean[None]) * rstd[None]
        pre = normed * gains[None] + shifts[None]
        value = pre / (1.0 + jnp.exp(-pre))
        if i == 0:
            value = value * top
        if i == rows - 1:
            value = value * bottom
        out[t, i] = value.reshape(values.shape).astype(BF16)

    return activate


def own_kernel(cot, above, below, weight, centre, act, gathered, gain, shift, out, longer, stats, raw, lefts, taps, acc, more, block, acts, tap_sem, more_sem, raw_sem, block_sem, acts_sem):
    frames, rows, cols, chans = act.shape
    load_act = pltpu.make_async_copy(act, raw, raw_sem)
    load_act.start()
    load_cot = [pltpu.make_async_copy(cot.at[:, h], block.at[h, 1], block_sem.at[h]) for h in range(rows)]
    for load in load_cot:
        load.start()
    fetches = [
        [pltpu.make_async_copy(weight.at[a, b], taps.at[a - 1, b], tap_sem.at[a - 1, b]) for a in (2, 1)]
        for b in (0, 2)
    ]
    for fetch in fetches[0]:
        fetch.start()
    load_more = pltpu.make_async_copy(centre, more, more_sem)
    entries = frames * rows * cols * (chans // GROUPS)
    mean, rstd = group_stats(gathered[...], entries, chans)
    stats[0] = mean
    stats[1] = rstd
    activate = activation(mean, rstd, gain, shift, acts)
    for t in range(frames):
        activate(above[0, t], t, 0)
        activate(below[0, t], t, rows + 1)
    load_act.wait()
    sends = [pltpu.make_async_copy(acts.at[t], longer.at[t], acts_sem.at[t]) for t in range(frames)]
    for load in load_cot:
        load.wait()
    fill_lefts((block.at[0], block.at[1]), above, below, lefts)

    def before(n):
        for fetch in fetches[n]:
            fetch.wait()
        if n == 0:
            for fetch in fetches[1]:
                fetch.start()
            load_more.start()
        else:
            for send in sends:
                send.start()

    def between(b, c):
        if b == 0 and c != 1:
            t = 0 if c == 0 else 1
            for h in range(rows):
                activate(raw[t, h], t, 1 + h)

    grad_products(1, 0, 1, 0, (lefts.at[0], lefts.at[1]), taps, acc, before, between)
    load_more.wait()
    finish(acc, out, 2, more)
    for send in sends:
        send.wait()


def sides(acc, earlier, later, frames_rows):
    positions, chans = acc.shape[1:]
    cols = positions // frames_rows
    col = lax.broadcasted_iota(jnp.int32, (cols, chans), 0)
    for n in range(frames_rows):
        at = slice(n * cols, (n + 1) * cols)
        before = jnp.where(col == 0, 0.0, pltpu.roll(acc[earlier, at], 1, 0))
        after = jnp.where(col == cols - 1, 0.0, pltpu.roll(acc[later, at], cols - 1, 0))
        acc[earlier, at] = before + after


def finish(acc, out, beside, more):
    frames, rows, cols, chans = out.shape
    for t in range(frames):
        for h in range(rows):
            at = slice((t * rows + h) * cols, (t * rows + h + 1) * cols)
            total = acc[beside, at] + acc[1, at]
            if more is not None:
                total = total + more[t, h]
            out[t, h] = total.astype(out.dtype)


def group_stats(gathered, entries, chans):
    parts = gathered.shape[0]
    count = parts * entries
    sums = jnp.sum(gathered, axis=0, keepdims=True)
    mean = sums / count
    apart = gathered * (1.0 / entries) - mean
    between = jnp.sum(apart * apart, axis=0, keepdims=True) * entries
    var = (between + second_part(sums)) / count
    lane = lax.broadcasted_iota(jnp.int32, (1, LANES), 1)
    rstd = jnp.where(lane < GROUPS, lax.rsqrt(jnp.where(lane < GROUPS, var, 1.0) + 1e-06), 0.0)
    return to_chans(mean, rstd, chans)


def point_kernel(own, incoming, act, stats, gain, shift, early, pre_grad, pay, block, extra, block_sem, extra_sem):
    frames, rows, cols, chans = act.shape
    mean, rstd = stats[0], stats[1]
    first = lax.axis_index("ta") == 0

    @pl.when(first)
    def _():
        load = pltpu.make_async_copy(early, extra, extra_sem)
        load.start()
        load.wait()
        for h in range(rows):
            block[0, h] = extra[0, h].astype(F32) + extra[1, h].astype(F32)

    @pl.when(jnp.logical_not(first))
    def _():
        block[0] = jnp.zeros_like(block[0])

    gains = jnp.broadcast_to(gain[...], (8, chans))
    shifts = jnp.broadcast_to(shift[...], (8, chans))
    shift_sum = jnp.zeros((8, chans), F32)
    gain_sum = jnp.zeros((8, chans), F32)
    sends = []
    for t in range(frames):
        for h in range(rows):
            grad = own[t, h] + incoming[t, h].astype(F32)
            if t == 0:
                grad = grad + block[0, h]
            normed = (eights(act[t, h].astype(F32)) - mean[None]) * rstd[None]
            pre = normed * gains[None] + shifts[None]
            sig = 1.0 / (1.0 + jnp.exp(-pre))
            local = eights(grad) * sig * (1.0 + pre * (1.0 - sig))
            block[t, h] = local.reshape(cols, chans)
            shift_sum = shift_sum + jnp.sum(local, axis=0)
            gain_sum = gain_sum + jnp.sum(local * normed, axis=0)
            sends.append(pltpu.make_async_copy(block.at[t, h], pre_grad.at[t, h], block_sem.at[t, h]))
            sends[-1].start()
    row = to_groups(gains * shift_sum, gains * gain_sum)
    pay[...] = jnp.broadcast_to(row, pay.shape)
    for send in sends:
        send.wait()


def conv_kernel(acts, prior, weight, stats, gain, shift, out, raw, ext, near, far, near_taps, far_taps, acc, raw_sem, ext_sem, near_sem, far_sem):
    frames, rows, cols, chans = out.shape
    positions = frames * rows * cols
    order = (0, 2, 1)
    first = lax.axis_index("ta") == 0
    load = pltpu.make_async_copy(prior, raw, raw_sem)
    load.start()
    own = pltpu.make_async_copy(acts, ext.at[frames:], ext_sem)
    own.start()
    fetches = [pltpu.make_async_copy(weight.at[2, :, c], near_taps.at[c], near_sem.at[c]) for c in order]
    fetches += [pltpu.make_async_copy(weight.at[0:2, :, c], far_taps.at[c], far_sem.at[c]) for c in order]
    fetches[0].start()
    fetches[1].start()
    activate = activation(stats[0], stats[1], gain, shift, ext)

    load.wait()

    @pl.when(jnp.logical_not(first))
    def _():
        for t in range(frames):
            for i in range(rows + 2):
                activate(raw[t, i], t, i)

    own.wait()

    @pl.when(first)
    def _():
        for t in range(frames):
            ext[t] = ext[frames]

    for b in range(3):
        near[:, :, :, b * chans : (b + 1) * chans] = ext[2 : 2 + frames, b : b + rows]
    left = near[...].reshape(positions, 3 * chans)
    for n, c in enumerate(order):
        fetches[n].wait()
        fetches[n + 2].start()
        acc[c] = jnp.dot(left, near_taps[c].reshape(3 * chans, chans), preferred_element_type=F32)
    for a in range(2):
        for b in range(3):
            k = (3 * a + b) * chans
            far[:, :, :, k : k + chans] = ext[a : a + frames, b : b + rows]
    left = far[...].reshape(positions, 6 * chans)
    for n, c in enumerate(order):
        fetches[3 + n].wait()
        if n == 0:
            fetches[5].start()
        if c == 1:
            sides(acc, 0, 2, frames * rows)
        acc[c] += jnp.dot(left, far_taps[c].reshape(6 * chans, chans), preferred_element_type=F32)
    finish(acc, out, 0, None)


def final_kernel(pre_grad, act, gathered, stats, gain, out, block, done, block_sem, done_sem):
    frames, rows, cols, chans = act.shape
    places = [(t, h) for t in range(frames) for h in range(rows)]
    loads = [pltpu.make_async_copy(pre_grad.at[at], block.at[at], block_sem.at[at]) for at in places]
    for load in loads:
        load.start()
    count = gathered.shape[0] * frames * rows * cols * (chans // GROUPS)
    sums = jnp.sum(gathered[...], axis=0, keepdims=True) / count
    first, second = to_chans(sums, second_part(sums), chans)
    mean, rstd = stats[0], stats[1]
    gains = jnp.broadcast_to(gain[...], (8, chans))
    sends = []
    for at, load in zip(places, loads):
        load.wait()
        normed = (eights(act[at].astype(F32)) - mean[None]) * rstd[None]
        value = rstd[None] * (eights(block[at]) * gains[None] - first[None] - normed * second[None])
        done[at] = value.reshape(cols, chans).astype(BF16)
        sends.append(pltpu.make_async_copy(done.at[at], out.at[at], done_sem.at[at]))
        sends[-1].start()
    for send in sends:
        send.wait()


def moved(value, frame_step, row_step):
    frames, rows = lax.axis_size("ta"), lax.axis_size("ha")
    pairs = []
    for t in range(frames):
        for h in range(rows):
            to_t, to_h = t + frame_step, h + row_step
            if 0 <= to_t < frames and 0 <= to_h < rows:
                pairs.append((t * rows + h, to_t * rows + to_h))
    return lax.ppermute(value, BOTH, pairs)


def in_hbm(value):
    return pltpu.with_memory_space_constraint(value, pltpu.HBM)


def in_vmem(value):
    return pltpu.with_memory_space_constraint(value, pltpu.VMEM)


def on_device(activations, gain, shift, weight, cotangent):
    shape = activations.shape
    frames, rows, cols, chans = shape
    act, cot, taps = in_hbm(activations), in_hbm(cotangent), in_hbm(weight)
    parts = lax.axis_size("ta") * lax.axis_size("ha")
    gain, shift = gain.reshape(1, chans), shift.reshape(1, chans)
    gathered_shape = jax.ShapeDtypeStruct((parts, LANES), F32)
    edge = jax.ShapeDtypeStruct((2, frames, cols, chans), BF16)
    longer_shape = (frames, rows + 2, cols, chans)
    positions = frames * rows * cols

    pay, up, down = pl.pallas_call(
        stats_kernel,
        in_specs=[HBM, HBM],
        out_specs=[WHOLE] * 3,
        out_shape=[gathered_shape, edge, edge],
        scratch_shapes=[DMA((frames, rows)), DMA((2,))],
        compiler_params=params(16),
    )(act, cot)
    above = moved(up, 0, 1)
    below = moved(down, 0, -1)
    gathered = lax.all_to_all(pay, BOTH, 0, 0, tiled=True)

    f32_block = jax.ShapeDtypeStruct(shape, F32)
    sums = (3, positions, chans)
    held, early_centre, own_centre = pl.pallas_call(
        centre_kernel,
        in_specs=[WHOLE, WHOLE, HBM],
        out_specs=[WHOLE, WHOLE, HBM],
        out_shape=[pltpu.VMEM(weight.shape, BF16), f32_block, pltpu.HBM(shape, F32)],
        scratch_shapes=[
            pltpu.VMEM(shape, BF16),
            pltpu.VMEM((2,) + sums, F32),
            pltpu.VMEM(shape, F32),
            DMA((3, 3)),
            DMA,
        ],
        compiler_params=params(16),
    )(up, down, taps)
    held = in_vmem(held)
    early, longer = pl.pallas_call(
        early_kernel,
        in_specs=[WHOLE] * 6,
        out_specs=[WHOLE, HBM],
        out_shape=[pltpu.VMEM(shape, BF16), pltpu.HBM(longer_shape, BF16)],
        scratch_shapes=[pltpu.VMEM((2,) + shape, BF16), pltpu.VMEM(sums, F32), DMA((frames, rows + 2))],
        compiler_params=params(16),
    )(up, down, above, below, held, early_centre)
    early, gathered = lax.optimization_barrier((early, gathered))
    incoming = moved(early, -1, 0)
    prior = moved(longer, 1, 0)
    own, acts, stats, act_held = pl.pallas_call(
        own_kernel,
        in_specs=[HBM, WHOLE, WHOLE, HBM, HBM, HBM, WHOLE, WHOLE, WHOLE],
        out_specs=[WHOLE, HBM, WHOLE, WHOLE],
        out_shape=[f32_block, pltpu.HBM(longer_shape, BF16), jax.ShapeDtypeStruct((2, 8, chans), F32), jax.ShapeDtypeStruct(shape, BF16)],
        scratch_shapes=[
            pltpu.VMEM((2,) + shape, BF16),
            pltpu.VMEM((2, 3, 3, chans, chans), BF16),
            pltpu.VMEM(sums, F32),
            pltpu.VMEM(shape, F32),
            pltpu.VMEM((rows, 2, frames, cols, chans), BF16),
            pltpu.VMEM(longer_shape, BF16),
            DMA((2, 3)),
            DMA,
            DMA,
            DMA((rows,)),
            DMA((frames,)),
        ],
        compiler_params=params(28),
    )(cot, above, below, taps, in_hbm(own_centre), act, gathered, gain, shift)
    pre_grad, pay = pl.pallas_call(
        point_kernel,
        in_specs=[WHOLE] * 6 + [ANY],
        out_specs=[HBM, WHOLE],
        out_shape=[pltpu.HBM(shape, F32), gathered_shape],
        scratch_shapes=[pltpu.VMEM(shape, F32), pltpu.VMEM(shape, BF16), DMA((frames, rows)), DMA],
        cost_estimate=pl.CostEstimate(flops=2 * 10**10, bytes_accessed=10**6, transcendentals=0),
        compiler_params=params(16),
    )(own, incoming, act_held, stats, gain, shift, early)
    gathered = lax.all_to_all(pay, BOTH, 0, 0, tiled=True)
    output = pl.pallas_call(
        conv_kernel,
        in_specs=[HBM, ANY, HBM, WHOLE, WHOLE, WHOLE],
        out_specs=WHOLE,
        out_shape=jax.ShapeDtypeStruct(shape, BF16),
        scratch_shapes=[
            pltpu.VMEM(longer_shape, BF16),
            pltpu.VMEM((frames + 2, rows + 2, cols, chans), BF16),
            pltpu.VMEM((frames, rows, cols, 3 * chans), BF16),
            pltpu.VMEM((frames, rows, cols, 6 * chans), BF16),
            pltpu.VMEM((3, 3, chans, chans), BF16),
            pltpu.VMEM((3, 2, 3, chans, chans), BF16),
            pltpu.VMEM(sums, F32),
            DMA,
            DMA,
            DMA((3,)),
            DMA((3,)),
        ],
        compiler_params=params(36),
    )(in_hbm(acts), prior, taps, stats, gain, shift)
    output, gathered = lax.optimization_barrier((output, gathered))
    input_grad = pl.pallas_call(
        final_kernel,
        in_specs=[HBM] + [WHOLE] * 4,
        out_specs=HBM,
        out_shape=pltpu.HBM(shape, BF16),
        scratch_shapes=[
            pltpu.VMEM(shape, F32),
            pltpu.VMEM(shape, BF16),
            DMA((frames, rows)),
            DMA((frames, rows)),
        ],
        compiler_params=params(16),
    )(in_hbm(pre_grad), activations, gathered, stats, gain)
    return (output, input_grad)


def solution(mesh):
    placed = (P("ta", "ha", None, None), P(), P(), P(), P("ta", "ha", None, None))
    return jax.shard_map(
        on_device,
        mesh=mesh,
        in_specs=placed,
        out_specs=(P("ta", "ha", None, None), P("ta", "ha", None, None)),
        check_vma=False,
    )
```

```python
import jax
import jax.numpy as jnp
from jax import lax
from jax.experimental import pallas as pl
from jax.experimental.pallas import tpu as pltpu
from jax.sharding import PartitionSpec as P

GROUPS = 32
LANES = 128
F32 = jnp.float32
BF16 = jnp.bfloat16
HBM = pl.BlockSpec(memory_space=pltpu.HBM)
ANY = pl.BlockSpec(memory_space=pl.ANY)
WHOLE = pl.BlockSpec(memory_space=pltpu.VMEM)
DMA = pltpu.SemaphoreType.DMA
BOTH = ("ta", "ha")


def params(mebibytes):
    return pltpu.CompilerParams(vmem_limit_bytes=mebibytes * 2**20)


def member(chans, across):
    shape, chan_dim = ((LANES, chans), 1) if across else ((chans, LANES), 0)
    per_group = chans // GROUPS
    chan = lax.broadcasted_iota(jnp.int32, shape, chan_dim)
    lane = lax.broadcasted_iota(jnp.int32, shape, 1 - chan_dim)
    inside = (chan >= lane * per_group) & (chan < (lane + 1) * per_group)
    return jnp.where(inside, 1.0, 0.0).astype(BF16)


def exact_dot(left, right):
    high = left.astype(BF16).astype(F32)
    rest = left - high
    middle = rest.astype(BF16).astype(F32)
    parts = jnp.concatenate([high, middle, rest - middle], axis=0).astype(BF16)
    out = jnp.dot(parts, right, preferred_element_type=F32)
    rows = left.shape[0]
    return out[2 * rows :] + out[rows : 2 * rows] + out[:rows]


def to_groups(one, two):
    lanes = exact_dot(jnp.concatenate([one, two], axis=0), member(one.shape[1], False))
    return jnp.sum(lanes[:8] + pltpu.roll(lanes[8:], GROUPS, 1), axis=0, keepdims=True)


def to_chans(one, two, chans):
    rows = jnp.concatenate([jnp.broadcast_to(one, (8, LANES)), jnp.broadcast_to(two, (8, LANES))], axis=0)
    out = exact_dot(rows, member(chans, True))
    return out[:8], out[8:]


def second_part(row):
    return pltpu.roll(jnp.broadcast_to(row, (8, LANES)), LANES - GROUPS, 1)[:1]


def eights(value):
    return value.reshape(value.shape[0] // 8, 8, value.shape[1])


def pack_kernel(act, cot, up, down, sem):
    packs = []
    for n, source in enumerate((act, cot)):
        for k, (h, side) in enumerate(((0, down), (act.shape[1] - 1, up))):
            packs.append(pltpu.make_async_copy(source.at[:, h], side.at[n], sem.at[n, k]))
            packs[-1].start()
    for pack in packs:
        pack.wait()


def stats_kernel(up, down, pay):
    frames, cols, chans = up.shape[1:]
    blocks = [(t, side) for t in range(frames) for side in (down, up)]
    entries = len(blocks) * cols * (chans // GROUPS)
    none = jnp.zeros((8, chans), F32)
    total = none
    for t, side in blocks:
        total = total + jnp.sum(eights(side[0, t].astype(F32)), axis=0)
    sums = to_groups(total, none)
    mean, _ = to_chans(sums / entries, sums, chans)
    spread = none
    for t, side in blocks:
        centered = eights(side[0, t].astype(F32)) - mean[None]
        spread = spread + jnp.sum(centered * centered, axis=0)
    pay[...] = jnp.broadcast_to(sums + to_groups(none, spread), pay.shape)


def centre_kernel(up, down, weight, taps, early, own, block, acc, late, tap_sem, late_sem):
    frames, cols, chans = up.shape[1:]
    rows = 2
    half = rows * cols
    order = [(2, 1), (1, 1), (0, 1), (0, 0), (0, 2), (1, 0), (1, 2)]
    fetches = [pltpu.make_async_copy(weight.at[a, b], taps.at[a, b], tap_sem.at[a, b]) for a, b in order]
    fetches[0].start()
    for t in range(frames):
        block[t, 0] = down[1, t]
        block[t, 1] = up[1, t]
    fetches[1].start()
    left = block[...].reshape(2 * half, chans)
    for n, a in enumerate((2, 1, 0)):
        fetches[n].wait()
        for fetch in (fetches[2:4], fetches[4:6], [])[n]:
            fetch.start()
        for c in (0, 2, 1):
            if a < 2 and c == 1:
                sides(acc.at[a], 2, 0, 2 * rows)
            term = transposed_dot(left, taps[a, 1, c])
            if a == 2:
                acc[1, c] = term
            elif a == 1:
                acc[1, c, :half] += term[half:]
                acc[0, c, half:] = term[:half]
            else:
                acc[0, c, :half] = term[:half]
                acc[0, c, half:] += term[half:]
        if a == 1:
            for fetch in fetches[6:]:
                fetch.start()
            finish(acc.at[1], late, 2, None)
            send = pltpu.make_async_copy(late, own, late_sem)
            send.start()
    finish(acc.at[0], early, 2, None)
    send.wait()
    for fetch in fetches[3:]:
        fetch.wait()


def transposed_dot(left, right):
    return lax.dot_general(left, right, (((1,), (1,)), ((), ())), preferred_element_type=F32)


def grad_products(full, part, source, target, lefts, taps, acc, before=None, between=None):
    half = lefts[0].shape[1] * lefts[0].shape[2]
    chans = lefts[0].shape[3]
    for n, b in enumerate((0, 2)):
        if before is not None:
            before(n)
        both = lefts[n][...].reshape(2 * half, chans)
        one = lefts[n][source].reshape(half, chans)
        for c in (0, 2, 1):
            if b == 2 and c == 1:
                sides(acc, 2, 0, half // lefts[0].shape[2] * 2)
            term = transposed_dot(both, taps[full, b, c])
            if b == 0:
                acc[c] = term
            else:
                acc[c] += term
            if between is not None:
                between(b, c)
            acc[c, target * half : (target + 1) * half] += transposed_dot(one, taps[part, b, c])


def fill_lefts(cot, above, below, lefts):
    for t in range(lefts.shape[1]):
        lefts[0, t, 0] = cot[1][1, t]
        lefts[0, t, 1] = below[1, t]
        lefts[1, t, 0] = above[1, t]
        lefts[1, t, 1] = cot[0][1, t]


def early_kernel(up, down, above, below, taps, centre, out, longer, lefts, acc, send_sem):
    sends = [
        pltpu.make_async_copy(side.at[0, t], longer.at[t, n], send_sem.at[t, n])
        for n, side in enumerate((above, down, up, below))
        for t in range(out.shape[0])
    ]
    for send in sends:
        send.start()
    fill_lefts((down, up), above, below, lefts)
    grad_products(0, 1, 0, 1, (lefts.at[0], lefts.at[1]), taps, acc)
    finish(acc, out, 2, centre)
    for send in sends:
        send.wait()


def activation(mean, rstd, gain, shift, out):
    chans, rows = out.shape[3], out.shape[1]
    gains = jnp.broadcast_to(gain[...], (8, chans))
    shifts = jnp.broadcast_to(shift[...], (8, chans))
    row_at = lax.axis_index("ha")
    last_row = lax.axis_size("ha") - 1
    top = jnp.where(row_at == 0, 0.0, 1.0).astype(F32)
    bottom = jnp.where(row_at == last_row, 0.0, 1.0).astype(F32)

    def activate(values, t, i):
        normed = (eights(values.astype(F32)) - mean[None]) * rstd[None]
        pre = normed * gains[None] + shifts[None]
        value = pre / (1.0 + jnp.exp(-pre))
        if i == 0:
            value = value * top
        if i == rows - 1:
            value = value * bottom
        out[t, i] = value.reshape(values.shape).astype(BF16)

    return activate


def own_kernel(cot, above, below, weight, centre, act, gathered, gain, shift, out, longer, stats, raw, lefts, taps, acc, more, block, acts, tap_sem, more_sem, raw_sem, block_sem, acts_sem):
    frames, rows, cols, chans = act.shape
    load_act = pltpu.make_async_copy(act, raw, raw_sem)
    load_act.start()
    load_cot = [pltpu.make_async_copy(cot.at[:, h], block.at[h, 1], block_sem.at[h]) for h in range(rows)]
    for load in load_cot:
        load.start()
    fetches = [
        [pltpu.make_async_copy(weight.at[a, b], taps.at[a - 1, b], tap_sem.at[a - 1, b]) for a in (2, 1)]
        for b in (0, 2)
    ]
    for fetch in fetches[0]:
        fetch.start()
    load_more = pltpu.make_async_copy(centre, more, more_sem)
    entries = frames * rows * cols * (chans // GROUPS)
    mean, rstd = group_stats(gathered[...], entries, chans)
    stats[0] = mean
    stats[1] = rstd
    activate = activation(mean, rstd, gain, shift, acts)
    for t in range(frames):
        activate(above[0, t], t, 0)
        activate(below[0, t], t, rows + 1)
    load_act.wait()
    sends = [pltpu.make_async_copy(acts.at[t], longer.at[t], acts_sem.at[t]) for t in range(frames)]
    for load in load_cot:
        load.wait()
    fill_lefts((block.at[0], block.at[1]), above, below, lefts)

    def before(n):
        for fetch in fetches[n]:
            fetch.wait()
        if n == 0:
            for fetch in fetches[1]:
                fetch.start()
            load_more.start()
        else:
            for send in sends:
                send.start()

    def between(b, c):
        if b == 0 and c != 1:
            t = 0 if c == 0 else 1
            for h in range(rows):
                activate(raw[t, h], t, 1 + h)

    grad_products(1, 0, 1, 0, (lefts.at[0], lefts.at[1]), taps, acc, before, between)
    load_more.wait()
    finish(acc, out, 2, more)
    for send in sends:
        send.wait()


def sides(acc, earlier, later, frames_rows):
    positions, chans = acc.shape[1:]
    cols = positions // frames_rows
    col = lax.broadcasted_iota(jnp.int32, (cols, chans), 0)
    for n in range(frames_rows):
        at = slice(n * cols, (n + 1) * cols)
        before = jnp.where(col == 0, 0.0, pltpu.roll(acc[earlier, at], 1, 0))
        after = jnp.where(col == cols - 1, 0.0, pltpu.roll(acc[later, at], cols - 1, 0))
        acc[earlier, at] = before + after


def finish(acc, out, beside, more):
    frames, rows, cols, chans = out.shape
    for t in range(frames):
        for h in range(rows):
            at = slice((t * rows + h) * cols, (t * rows + h + 1) * cols)
            total = acc[beside, at] + acc[1, at]
            if more is not None:
                total = total + more[t, h]
            out[t, h] = total.astype(out.dtype)


def group_stats(gathered, entries, chans):
    parts = gathered.shape[0]
    count = parts * entries
    sums = jnp.sum(gathered, axis=0, keepdims=True)
    mean = sums / count
    apart = gathered * (1.0 / entries) - mean
    between = jnp.sum(apart * apart, axis=0, keepdims=True) * entries
    var = (between + second_part(sums)) / count
    lane = lax.broadcasted_iota(jnp.int32, (1, LANES), 1)
    rstd = jnp.where(lane < GROUPS, lax.rsqrt(jnp.where(lane < GROUPS, var, 1.0) + 1e-06), 0.0)
    return to_chans(mean, rstd, chans)


def point_kernel(own, incoming, act, stats, gain, shift, early, pre_grad, pay, block, extra, block_sem, extra_sem):
    frames, rows, cols, chans = act.shape
    mean, rstd = stats[0], stats[1]
    first = lax.axis_index("ta") == 0

    @pl.when(first)
    def _():
        load = pltpu.make_async_copy(early, extra, extra_sem)
        load.start()
        load.wait()
        for h in range(rows):
            block[0, h] = extra[0, h].astype(F32) + extra[1, h].astype(F32)

    @pl.when(jnp.logical_not(first))
    def _():
        block[0] = jnp.zeros_like(block[0])

    gains = jnp.broadcast_to(gain[...], (8, chans))
    shifts = jnp.broadcast_to(shift[...], (8, chans))
    shift_sum = jnp.zeros((8, chans), F32)
    gain_sum = jnp.zeros((8, chans), F32)
    sends = []
    for t in range(frames):
        for h in range(rows):
            grad = own[t, h] + incoming[t, h].astype(F32)
            if t == 0:
                grad = grad + block[0, h]
            normed = (eights(act[t, h].astype(F32)) - mean[None]) * rstd[None]
            pre = normed * gains[None] + shifts[None]
            sig = 1.0 / (1.0 + jnp.exp(-pre))
            local = eights(grad) * sig * (1.0 + pre * (1.0 - sig))
            block[t, h] = local.reshape(cols, chans)
            shift_sum = shift_sum + jnp.sum(local, axis=0)
            gain_sum = gain_sum + jnp.sum(local * normed, axis=0)
            sends.append(pltpu.make_async_copy(block.at[t, h], pre_grad.at[t, h], block_sem.at[t, h]))
            sends[-1].start()
    row = to_groups(gains * shift_sum, gains * gain_sum)
    pay[...] = jnp.broadcast_to(row, pay.shape)
    for send in sends:
        send.wait()


def conv_kernel(acts, prior, weight, stats, gain, shift, out, ext, near, far, near_taps, far_taps, acc, ext_sem, near_sem, far_sem):
    frames, rows, cols, chans = out.shape
    positions = frames * rows * cols
    order = (0, 2, 1)
    first = lax.axis_index("ta") == 0
    own = pltpu.make_async_copy(acts, ext.at[frames:], ext_sem)
    own.start()
    fetches = [pltpu.make_async_copy(weight.at[2, :, c], near_taps.at[c], near_sem.at[c]) for c in order]
    fetches += [pltpu.make_async_copy(weight.at[0:2, :, c], far_taps.at[c], far_sem.at[c]) for c in order]
    fetches[0].start()
    activate = activation(stats[0], stats[1], gain, shift, ext)

    @pl.when(jnp.logical_not(first))
    def _():
        for t in range(frames):
            for i in range(rows + 2):
                activate(prior[t, i], t, i)

    own.wait()
    fetches[1].start()
    fetches[2].start()

    @pl.when(first)
    def _():
        for t in range(frames):
            ext[t] = ext[frames]

    for b in range(3):
        near[:, :, :, b * chans : (b + 1) * chans] = ext[2 : 2 + frames, b : b + rows]
    left = near[...].reshape(positions, 3 * chans)
    for n, c in enumerate(order):
        if n == 0:
            fetches[0].wait()
            fetches[3].start()
        if n == 1:
            fetches[1].wait()
            fetches[2].wait()
            fetches[4].start()
            fetches[5].start()
        acc[c] = jnp.dot(left, near_taps[c].reshape(3 * chans, chans), preferred_element_type=F32)
    for a in range(2):
        for b in range(3):
            k = (3 * a + b) * chans
            far[:, :, :, k : k + chans] = ext[a : a + frames, b : b + rows]
    left = far[...].reshape(positions, 6 * chans)
    for n, c in enumerate(order):
        if n == 0:
            fetches[3].wait()
        if n == 1:
            fetches[4].wait()
            fetches[5].wait()
        if c == 1:
            sides(acc, 0, 2, frames * rows)
        acc[c] += jnp.dot(left, far_taps[c].reshape(6 * chans, chans), preferred_element_type=F32)
    finish(acc, out, 0, None)


def final_kernel(pre_grad, act, gathered, stats, gain, out, block, raw, done, block_sem, raw_sem, done_sem):
    frames, rows, cols, chans = act.shape
    places = [(t, h) for t in range(frames) for h in range(rows)]
    loads = [
        (
            pltpu.make_async_copy(act.at[at], raw.at[at], raw_sem.at[at]),
            pltpu.make_async_copy(pre_grad.at[at], block.at[at], block_sem.at[at]),
        )
        for at in places
    ]
    for pair in loads:
        for load in pair:
            load.start()
    count = gathered.shape[0] * frames * rows * cols * (chans // GROUPS)
    sums = jnp.sum(gathered[...], axis=0, keepdims=True) / count
    first, second = to_chans(sums, second_part(sums), chans)
    mean, rstd = stats[0], stats[1]
    gains = jnp.broadcast_to(gain[...], (8, chans))
    sends = []
    for at, pair in zip(places, loads):
        for load in pair:
            load.wait()
        normed = (eights(raw[at].astype(F32)) - mean[None]) * rstd[None]
        value = rstd[None] * (eights(block[at]) * gains[None] - first[None] - normed * second[None])
        done[at] = value.reshape(cols, chans).astype(BF16)
        sends.append(pltpu.make_async_copy(done.at[at], out.at[at], done_sem.at[at]))
        sends[-1].start()
    for send in sends:
        send.wait()


def moved(value, frame_step, row_step):
    frames, rows = lax.axis_size("ta"), lax.axis_size("ha")
    pairs = []
    for t in range(frames):
        for h in range(rows):
            to_t, to_h = t + frame_step, h + row_step
            if 0 <= to_t < frames and 0 <= to_h < rows:
                pairs.append((t * rows + h, to_t * rows + to_h))
    return lax.ppermute(value, BOTH, pairs)


def in_hbm(value):
    return pltpu.with_memory_space_constraint(value, pltpu.HBM)


def in_vmem(value):
    return pltpu.with_memory_space_constraint(value, pltpu.VMEM)


def on_device(activations, gain, shift, weight, cotangent):
    shape = activations.shape
    frames, rows, cols, chans = shape
    act, cot, taps = in_hbm(activations), in_hbm(cotangent), in_hbm(weight)
    parts = lax.axis_size("ta") * lax.axis_size("ha")
    gain, shift = gain.reshape(1, chans), shift.reshape(1, chans)
    gathered_shape = jax.ShapeDtypeStruct((parts, LANES), F32)
    edge = jax.ShapeDtypeStruct((2, frames, cols, chans), BF16)
    longer_shape = (frames, rows + 2, cols, chans)
    positions = frames * rows * cols

    up, down = pl.pallas_call(
        pack_kernel,
        in_specs=[HBM, HBM],
        out_specs=[WHOLE] * 2,
        out_shape=[edge, edge],
        scratch_shapes=[DMA((2, 2))],
        compiler_params=params(16),
    )(act, cot)
    pay = pl.pallas_call(
        stats_kernel,
        in_specs=[WHOLE] * 2,
        out_specs=WHOLE,
        out_shape=gathered_shape,
        compiler_params=params(16),
    )(up, down)
    above = moved(up, 0, 1)
    below = moved(down, 0, -1)
    gathered = lax.all_to_all(pay, BOTH, 0, 0, tiled=True)

    f32_block = jax.ShapeDtypeStruct(shape, F32)
    sums = (3, positions, chans)
    held, early_centre, own_centre = pl.pallas_call(
        centre_kernel,
        in_specs=[WHOLE, WHOLE, HBM],
        out_specs=[WHOLE, WHOLE, HBM],
        out_shape=[pltpu.VMEM(weight.shape, BF16), f32_block, pltpu.HBM(shape, F32)],
        scratch_shapes=[
            pltpu.VMEM(shape, BF16),
            pltpu.VMEM((2,) + sums, F32),
            pltpu.VMEM(shape, F32),
            DMA((3, 3)),
            DMA,
        ],
        compiler_params=params(16),
    )(up, down, taps)
    held = in_vmem(held)
    early, longer = pl.pallas_call(
        early_kernel,
        in_specs=[WHOLE] * 6,
        out_specs=[WHOLE, HBM],
        out_shape=[pltpu.VMEM(shape, BF16), pltpu.HBM(longer_shape, BF16)],
        scratch_shapes=[pltpu.VMEM((2,) + shape, BF16), pltpu.VMEM(sums, F32), DMA((frames, rows + 2))],
        compiler_params=params(16),
    )(up, down, above, below, held, early_centre)
    early, gathered = lax.optimization_barrier((early, gathered))
    incoming = moved(early, -1, 0)
    prior = moved(longer, 1, 0)
    own, acts, stats, act_held = pl.pallas_call(
        own_kernel,
        in_specs=[HBM, WHOLE, WHOLE, HBM, HBM, HBM, WHOLE, WHOLE, WHOLE],
        out_specs=[WHOLE, HBM, WHOLE, WHOLE],
        out_shape=[f32_block, pltpu.HBM(longer_shape, BF16), jax.ShapeDtypeStruct((2, 8, chans), F32), jax.ShapeDtypeStruct(shape, BF16)],
        scratch_shapes=[
            pltpu.VMEM((2,) + shape, BF16),
            pltpu.VMEM((2, 3, 3, chans, chans), BF16),
            pltpu.VMEM(sums, F32),
            pltpu.VMEM(shape, F32),
            pltpu.VMEM((rows, 2, frames, cols, chans), BF16),
            pltpu.VMEM(longer_shape, BF16),
            DMA((2, 3)),
            DMA,
            DMA,
            DMA((rows,)),
            DMA((frames,)),
        ],
        compiler_params=params(28),
    )(cot, above, below, taps, in_hbm(own_centre), act, gathered, gain, shift)
    pre_grad, pay = pl.pallas_call(
        point_kernel,
        in_specs=[WHOLE] * 6 + [ANY],
        out_specs=[HBM, WHOLE],
        out_shape=[pltpu.HBM(shape, F32), gathered_shape],
        scratch_shapes=[pltpu.VMEM(shape, F32), pltpu.VMEM(shape, BF16), DMA((frames, rows)), DMA],
        cost_estimate=pl.CostEstimate(flops=2 * 10**10, bytes_accessed=10**6, transcendentals=0),
        compiler_params=params(16),
    )(own, incoming, act_held, stats, gain, shift, early)
    gathered = lax.all_to_all(pay, BOTH, 0, 0, tiled=True)
    output = pl.pallas_call(
        conv_kernel,
        in_specs=[HBM, WHOLE, HBM, WHOLE, WHOLE, WHOLE],
        out_specs=WHOLE,
        out_shape=jax.ShapeDtypeStruct(shape, BF16),
        scratch_shapes=[
            pltpu.VMEM((frames + 2, rows + 2, cols, chans), BF16),
            pltpu.VMEM((frames, rows, cols, 3 * chans), BF16),
            pltpu.VMEM((frames, rows, cols, 6 * chans), BF16),
            pltpu.VMEM((3, 3, chans, chans), BF16),
            pltpu.VMEM((3, 2, 3, chans, chans), BF16),
            pltpu.VMEM(sums, F32),
            DMA,
            DMA((3,)),
            DMA((3,)),
        ],
        compiler_params=params(36),
    )(in_hbm(acts), prior, taps, stats, gain, shift)
    output, gathered = lax.optimization_barrier((output, gathered))
    input_grad = pl.pallas_call(
        final_kernel,
        in_specs=[HBM, HBM, WHOLE, WHOLE, WHOLE],
        out_specs=HBM,
        out_shape=pltpu.HBM(shape, BF16),
        scratch_shapes=[
            pltpu.VMEM(shape, F32),
            pltpu.VMEM(shape, BF16),
            pltpu.VMEM(shape, BF16),
            DMA((frames, rows)),
            DMA((frames, rows)),
            DMA((frames, rows)),
        ],
        compiler_params=params(16),
    )(in_hbm(pre_grad), act, gathered, stats, gain)
    return (output, input_grad)


def solution(mesh):
    placed = (P("ta", "ha", None, None), P(), P(), P(), P("ta", "ha", None, None))
    return jax.shard_map(
        on_device,
        mesh=mesh,
        in_specs=placed,
        out_specs=(P("ta", "ha", None, None), P("ta", "ha", None, None)),
        check_vma=False,
    )
```

```python
import jax
import jax.numpy as jnp
from jax import lax
from jax.experimental import pallas as pl
from jax.experimental.pallas import tpu as pltpu
from jax.sharding import PartitionSpec as P

GROUPS = 32
LANES = 128
F32 = jnp.float32
BF16 = jnp.bfloat16
HBM = pl.BlockSpec(memory_space=pltpu.HBM)
ANY = pl.BlockSpec(memory_space=pl.ANY)
WHOLE = pl.BlockSpec(memory_space=pltpu.VMEM)
DMA = pltpu.SemaphoreType.DMA
BOTH = ("ta", "ha")


def params(mebibytes):
    return pltpu.CompilerParams(vmem_limit_bytes=mebibytes * 2**20)


def member(chans, across):
    shape, chan_dim = ((LANES, chans), 1) if across else ((chans, LANES), 0)
    per_group = chans // GROUPS
    chan = lax.broadcasted_iota(jnp.int32, shape, chan_dim)
    lane = lax.broadcasted_iota(jnp.int32, shape, 1 - chan_dim)
    inside = (chan >= lane * per_group) & (chan < (lane + 1) * per_group)
    return jnp.where(inside, 1.0, 0.0).astype(BF16)


def exact_dot(left, right):
    high = left.astype(BF16).astype(F32)
    rest = left - high
    middle = rest.astype(BF16).astype(F32)
    parts = jnp.concatenate([high, middle, rest - middle], axis=0).astype(BF16)
    out = jnp.dot(parts, right, preferred_element_type=F32)
    rows = left.shape[0]
    return out[2 * rows :] + out[rows : 2 * rows] + out[:rows]


def to_groups(one, two):
    lanes = exact_dot(jnp.concatenate([one, two], axis=0), member(one.shape[1], False))
    return jnp.sum(lanes[:8] + pltpu.roll(lanes[8:], GROUPS, 1), axis=0, keepdims=True)


def to_chans(one, two, chans):
    rows = jnp.concatenate([jnp.broadcast_to(one, (8, LANES)), jnp.broadcast_to(two, (8, LANES))], axis=0)
    out = exact_dot(rows, member(chans, True))
    return out[:8], out[8:]


def second_part(row):
    return pltpu.roll(jnp.broadcast_to(row, (8, LANES)), LANES - GROUPS, 1)[:1]


def eights(value):
    return value.reshape(value.shape[0] // 8, 8, value.shape[1])


def pack_kernel(act, cot, up, down, sem):
    packs = []
    for n, source in enumerate((act, cot)):
        for k, (h, side) in enumerate(((0, down), (act.shape[1] - 1, up))):
            packs.append(pltpu.make_async_copy(source.at[:, h], side.at[n], sem.at[n, k]))
            packs[-1].start()
    for pack in packs:
        pack.wait()


def stats_kernel(up, down, pay):
    frames, cols, chans = up.shape[1:]
    blocks = [(t, side) for t in range(frames) for side in (down, up)]
    entries = len(blocks) * cols * (chans // GROUPS)
    none = jnp.zeros((8, chans), F32)
    total = none
    for t, side in blocks:
        total = total + jnp.sum(eights(side[0, t].astype(F32)), axis=0)
    sums = to_groups(total, none)
    mean, _ = to_chans(sums / entries, sums, chans)
    spread = none
    for t, side in blocks:
        centered = eights(side[0, t].astype(F32)) - mean[None]
        spread = spread + jnp.sum(centered * centered, axis=0)
    pay[...] = jnp.broadcast_to(sums + to_groups(none, spread), pay.shape)


def centre_kernel(up, down, weight, taps, early, own, block, acc, late, tap_sem, late_sem):
    frames, cols, chans = up.shape[1:]
    rows = 2
    half = rows * cols
    order = [(2, 1), (1, 1), (0, 1), (0, 0), (0, 2), (1, 0), (1, 2)]
    fetches = [pltpu.make_async_copy(weight.at[a, b], taps.at[a, b], tap_sem.at[a, b]) for a, b in order]
    fetches[0].start()
    for t in range(frames):
        block[t, 0] = down[1, t]
        block[t, 1] = up[1, t]
    fetches[1].start()
    left = block[...].reshape(2 * half, chans)
    for n, a in enumerate((2, 1, 0)):
        fetches[n].wait()
        for fetch in (fetches[2:4], fetches[4:6], [])[n]:
            fetch.start()
        for c in (0, 2, 1):
            if a < 2 and c == 1:
                sides(acc.at[a], 2, 0, 2 * rows)
            term = transposed_dot(left, taps[a, 1, c])
            if a == 2:
                acc[1, c] = term
            elif a == 1:
                acc[1, c, :half] += term[half:]
                acc[0, c, half:] = term[:half]
            else:
                acc[0, c, :half] = term[:half]
                acc[0, c, half:] += term[half:]
        if a == 1:
            for fetch in fetches[6:]:
                fetch.start()
            finish(acc.at[1], late, 2, None)
            send = pltpu.make_async_copy(late, own, late_sem)
            send.start()
    finish(acc.at[0], early, 2, None)
    send.wait()
    for fetch in fetches[3:]:
        fetch.wait()


def transposed_dot(left, right):
    return lax.dot_general(left, right, (((1,), (1,)), ((), ())), preferred_element_type=F32)


def grad_products(full, part, source, target, lefts, taps, acc, before=None, between=None):
    half = lefts[0].shape[1] * lefts[0].shape[2]
    chans = lefts[0].shape[3]
    for n, b in enumerate((0, 2)):
        if before is not None:
            before(n)
        both = lefts[n][...].reshape(2 * half, chans)
        one = lefts[n][source].reshape(half, chans)
        for c in (0, 2, 1):
            if b == 2 and c == 1:
                sides(acc, 2, 0, half // lefts[0].shape[2] * 2)
            term = transposed_dot(both, taps[full, b, c])
            if b == 0:
                acc[c] = term
            else:
                acc[c] += term
            if between is not None:
                between(b, c)
            acc[c, target * half : (target + 1) * half] += transposed_dot(one, taps[part, b, c])


def fill_lefts(cot, above, below, lefts):
    for t in range(lefts.shape[1]):
        lefts[0, t, 0] = cot[1][1, t]
        lefts[0, t, 1] = below[1, t]
        lefts[1, t, 0] = above[1, t]
        lefts[1, t, 1] = cot[0][1, t]


def early_kernel(up, down, above, below, taps, centre, out, longer, lefts, acc, send_sem):
    sends = [
        pltpu.make_async_copy(side.at[0, t], longer.at[t, n], send_sem.at[t, n])
        for n, side in enumerate((above, down, up, below))
        for t in range(out.shape[0])
    ]
    for send in sends:
        send.start()
    fill_lefts((down, up), above, below, lefts)
    grad_products(0, 1, 0, 1, (lefts.at[0], lefts.at[1]), taps, acc)
    finish(acc, out, 2, centre)
    for send in sends:
        send.wait()


def activation(mean, rstd, gain, shift, out):
    chans, rows = out.shape[3], out.shape[1]
    gains = jnp.broadcast_to(gain[...], (8, chans))
    shifts = jnp.broadcast_to(shift[...], (8, chans))
    row_at = lax.axis_index("ha")
    last_row = lax.axis_size("ha") - 1
    top = jnp.where(row_at == 0, 0.0, 1.0).astype(F32)
    bottom = jnp.where(row_at == last_row, 0.0, 1.0).astype(F32)

    def activate(values, t, i):
        normed = (eights(values.astype(F32)) - mean[None]) * rstd[None]
        pre = normed * gains[None] + shifts[None]
        value = pre / (1.0 + jnp.exp(-pre))
        if i == 0:
            value = value * top
        if i == rows - 1:
            value = value * bottom
        out[t, i] = value.reshape(values.shape).astype(BF16)

    return activate


def own_kernel(cot, above, below, weight, centre, act, gathered, gain, shift, out, longer, stats, raw, lefts, taps, acc, more, block, acts, tap_sem, more_sem, raw_sem, block_sem, acts_sem):
    frames, rows, cols, chans = act.shape
    load_act = pltpu.make_async_copy(act, raw, raw_sem)
    load_act.start()
    load_cot = [pltpu.make_async_copy(cot.at[:, h], block.at[h, 1], block_sem.at[h]) for h in range(rows)]
    for load in load_cot:
        load.start()
    fetches = [
        [pltpu.make_async_copy(weight.at[a, b], taps.at[a - 1, b], tap_sem.at[a - 1, b]) for a in (2, 1)]
        for b in (0, 2)
    ]
    for fetch in fetches[0]:
        fetch.start()
    load_more = pltpu.make_async_copy(centre, more, more_sem)
    entries = frames * rows * cols * (chans // GROUPS)
    mean, rstd = group_stats(gathered[...], entries, chans)
    stats[0] = mean
    stats[1] = rstd
    activate = activation(mean, rstd, gain, shift, acts)
    for t in range(frames):
        activate(above[0, t], t, 0)
        activate(below[0, t], t, rows + 1)
    load_act.wait()
    sends = [pltpu.make_async_copy(acts.at[t], longer.at[t], acts_sem.at[t]) for t in range(frames)]
    for load in load_cot:
        load.wait()
    fill_lefts((block.at[0], block.at[1]), above, below, lefts)

    def before(n):
        for fetch in fetches[n]:
            fetch.wait()
        if n == 0:
            for fetch in fetches[1]:
                fetch.start()
            load_more.start()
        else:
            for send in sends:
                send.start()

    def between(b, c):
        if b == 0 and c != 1:
            t = 0 if c == 0 else 1
            for h in range(rows):
                activate(raw[t, h], t, 1 + h)

    grad_products(1, 0, 1, 0, (lefts.at[0], lefts.at[1]), taps, acc, before, between)
    load_more.wait()
    finish(acc, out, 2, more)
    for send in sends:
        send.wait()


def sides(acc, earlier, later, frames_rows):
    positions, chans = acc.shape[1:]
    cols = positions // frames_rows
    col = lax.broadcasted_iota(jnp.int32, (cols, chans), 0)
    for n in range(frames_rows):
        at = slice(n * cols, (n + 1) * cols)
        before = jnp.where(col == 0, 0.0, pltpu.roll(acc[earlier, at], 1, 0))
        after = jnp.where(col == cols - 1, 0.0, pltpu.roll(acc[later, at], cols - 1, 0))
        acc[earlier, at] = before + after


def finish(acc, out, beside, more):
    frames, rows, cols, chans = out.shape
    for t in range(frames):
        for h in range(rows):
            at = slice((t * rows + h) * cols, (t * rows + h + 1) * cols)
            total = acc[beside, at] + acc[1, at]
            if more is not None:
                total = total + more[t, h]
            out[t, h] = total.astype(out.dtype)


def group_stats(gathered, entries, chans):
    parts = gathered.shape[0]
    count = parts * entries
    sums = jnp.sum(gathered, axis=0, keepdims=True)
    mean = sums / count
    apart = gathered * (1.0 / entries) - mean
    between = jnp.sum(apart * apart, axis=0, keepdims=True) * entries
    var = (between + second_part(sums)) / count
    lane = lax.broadcasted_iota(jnp.int32, (1, LANES), 1)
    rstd = jnp.where(lane < GROUPS, lax.rsqrt(jnp.where(lane < GROUPS, var, 1.0) + 1e-06), 0.0)
    return to_chans(mean, rstd, chans)


def point_kernel(own, incoming, act, stats, gain, shift, early, pre_grad, pay, block, extra, row_out, block_sem, extra_sem, row_sem):
    frames, rows, cols, chans = act.shape
    mean, rstd = stats[0], stats[1]
    first = lax.axis_index("ta") == 0

    @pl.when(first)
    def _():
        load = pltpu.make_async_copy(early, extra, extra_sem)
        load.start()
        load.wait()
        for h in range(rows):
            block[0, h] = extra[0, h].astype(F32) + extra[1, h].astype(F32)

    @pl.when(jnp.logical_not(first))
    def _():
        block[0] = jnp.zeros_like(block[0])

    gains = jnp.broadcast_to(gain[...], (8, chans))
    shifts = jnp.broadcast_to(shift[...], (8, chans))
    shift_sum = jnp.zeros((8, chans), F32)
    gain_sum = jnp.zeros((8, chans), F32)
    sends = []
    for t in range(frames):
        for h in range(rows):
            grad = own[t, h] + incoming[t, h].astype(F32)
            if t == 0:
                grad = grad + block[0, h]
            normed = (eights(act[t, h].astype(F32)) - mean[None]) * rstd[None]
            pre = normed * gains[None] + shifts[None]
            sig = 1.0 / (1.0 + jnp.exp(-pre))
            local = eights(grad) * sig * (1.0 + pre * (1.0 - sig))
            block[t, h] = local.reshape(cols, chans)
            shift_sum = shift_sum + jnp.sum(local, axis=0)
            gain_sum = gain_sum + jnp.sum(local * normed, axis=0)
            sends.append(pltpu.make_async_copy(block.at[t, h], pre_grad.at[t, h], block_sem.at[t, h]))
            sends[-1].start()
    row = to_groups(gains * shift_sum, gains * gain_sum)
    row_out[...] = jnp.broadcast_to(row, pay.shape)
    sends.append(pltpu.make_async_copy(row_out, pay, row_sem))
    sends[-1].start()
    for send in sends:
        send.wait()


def conv_kernel(acts, prior, weight, stats, gain, shift, act, out, held, ext, near, far, near_taps, far_taps, acc, ext_sem, near_sem, far_sem, held_sem):
    frames, rows, cols, chans = out.shape
    positions = frames * rows * cols
    order = (0, 2, 1)
    first = lax.axis_index("ta") == 0
    own = pltpu.make_async_copy(acts, ext.at[frames:], ext_sem)
    own.start()
    fetches = [pltpu.make_async_copy(weight.at[2, :, c], near_taps.at[c], near_sem.at[c]) for c in order]
    fetches += [pltpu.make_async_copy(weight.at[0:2, :, c], far_taps.at[c], far_sem.at[c]) for c in order]
    fetches[0].start()
    activate = activation(stats[0], stats[1], gain, shift, ext)

    @pl.when(jnp.logical_not(first))
    def _():
        for t in range(frames):
            for i in range(rows + 2):
                activate(prior[t, i], t, i)

    own.wait()
    fetches[1].start()
    fetches[2].start()

    @pl.when(first)
    def _():
        for t in range(frames):
            ext[t] = ext[frames]

    for b in range(3):
        near[:, :, :, b * chans : (b + 1) * chans] = ext[2 : 2 + frames, b : b + rows]
    left = near[...].reshape(positions, 3 * chans)
    for n, c in enumerate(order):
        if n == 0:
            fetches[0].wait()
            fetches[3].start()
        if n == 1:
            fetches[1].wait()
            fetches[2].wait()
            fetches[4].start()
            fetches[5].start()
        acc[c] = jnp.dot(left, near_taps[c].reshape(3 * chans, chans), preferred_element_type=F32)
    for a in range(2):
        for b in range(3):
            k = (3 * a + b) * chans
            far[:, :, :, k : k + chans] = ext[a : a + frames, b : b + rows]
    left = far[...].reshape(positions, 6 * chans)
    for n, c in enumerate(order):
        if n == 0:
            fetches[3].wait()
            hold = pltpu.make_async_copy(act, held, held_sem)
            hold.start()
        if n == 1:
            fetches[4].wait()
            fetches[5].wait()
        if c == 1:
            sides(acc, 0, 2, frames * rows)
        acc[c] += jnp.dot(left, far_taps[c].reshape(6 * chans, chans), preferred_element_type=F32)
    finish(acc, out, 0, None)
    hold.wait()


def final_kernel(pre_grad, act, gathered, stats, gain, out, block, done, block_sem, done_sem):
    frames, rows, cols, chans = act.shape
    places = [(t, h) for t in range(frames) for h in range(rows)]
    loads = [pltpu.make_async_copy(pre_grad.at[at], block.at[at], block_sem.at[at]) for at in places]
    for load in loads:
        load.start()
    count = gathered.shape[0] * frames * rows * cols * (chans // GROUPS)
    sums = jnp.sum(gathered[...], axis=0, keepdims=True) / count
    first, second = to_chans(sums, second_part(sums), chans)
    mean, rstd = stats[0], stats[1]
    gains = jnp.broadcast_to(gain[...], (8, chans))
    sends = []
    for at, load in zip(places, loads):
        load.wait()
        normed = (eights(act[at].astype(F32)) - mean[None]) * rstd[None]
        value = rstd[None] * (eights(block[at]) * gains[None] - first[None] - normed * second[None])
        done[at] = value.reshape(cols, chans).astype(BF16)
        sends.append(pltpu.make_async_copy(done.at[at], out.at[at], done_sem.at[at]))
        sends[-1].start()
    for send in sends:
        send.wait()


def moved(value, frame_step, row_step):
    frames, rows = lax.axis_size("ta"), lax.axis_size("ha")
    pairs = []
    for t in range(frames):
        for h in range(rows):
            to_t, to_h = t + frame_step, h + row_step
            if 0 <= to_t < frames and 0 <= to_h < rows:
                pairs.append((t * rows + h, to_t * rows + to_h))
    return lax.ppermute(value, BOTH, pairs)


def in_hbm(value):
    return pltpu.with_memory_space_constraint(value, pltpu.HBM)


def in_vmem(value):
    return pltpu.with_memory_space_constraint(value, pltpu.VMEM)


def on_device(activations, gain, shift, weight, cotangent):
    shape = activations.shape
    frames, rows, cols, chans = shape
    act, cot, taps = in_hbm(activations), in_hbm(cotangent), in_hbm(weight)
    parts = lax.axis_size("ta") * lax.axis_size("ha")
    gain, shift = gain.reshape(1, chans), shift.reshape(1, chans)
    gathered_shape = jax.ShapeDtypeStruct((parts, LANES), F32)
    edge = jax.ShapeDtypeStruct((2, frames, cols, chans), BF16)
    longer_shape = (frames, rows + 2, cols, chans)
    positions = frames * rows * cols

    up, down = pl.pallas_call(
        pack_kernel,
        in_specs=[HBM, HBM],
        out_specs=[WHOLE] * 2,
        out_shape=[edge, edge],
        scratch_shapes=[DMA((2, 2))],
        compiler_params=params(16),
    )(act, cot)
    pay = pl.pallas_call(
        stats_kernel,
        in_specs=[WHOLE] * 2,
        out_specs=WHOLE,
        out_shape=gathered_shape,
        compiler_params=params(16),
    )(up, down)
    above = moved(up, 0, 1)
    below = moved(down, 0, -1)
    gathered = lax.all_to_all(pay, BOTH, 0, 0, tiled=True)

    f32_block = jax.ShapeDtypeStruct(shape, F32)
    sums = (3, positions, chans)
    held, early_centre, own_centre = pl.pallas_call(
        centre_kernel,
        in_specs=[WHOLE, WHOLE, HBM],
        out_specs=[WHOLE, WHOLE, HBM],
        out_shape=[pltpu.VMEM(weight.shape, BF16), f32_block, pltpu.HBM(shape, F32)],
        scratch_shapes=[
            pltpu.VMEM(shape, BF16),
            pltpu.VMEM((2,) + sums, F32),
            pltpu.VMEM(shape, F32),
            DMA((3, 3)),
            DMA,
        ],
        compiler_params=params(16),
    )(up, down, taps)
    held = in_vmem(held)
    early, longer = pl.pallas_call(
        early_kernel,
        in_specs=[WHOLE] * 6,
        out_specs=[WHOLE, HBM],
        out_shape=[pltpu.VMEM(shape, BF16), pltpu.HBM(longer_shape, BF16)],
        scratch_shapes=[pltpu.VMEM((2,) + shape, BF16), pltpu.VMEM(sums, F32), DMA((frames, rows + 2))],
        compiler_params=params(16),
    )(up, down, above, below, held, early_centre)
    early, gathered = lax.optimization_barrier((early, gathered))
    incoming = moved(early, -1, 0)
    prior = moved(longer, 1, 0)
    own, acts, stats, act_held = pl.pallas_call(
        own_kernel,
        in_specs=[HBM, WHOLE, WHOLE, HBM, HBM, HBM, WHOLE, WHOLE, WHOLE],
        out_specs=[WHOLE, HBM, WHOLE, WHOLE],
        out_shape=[f32_block, pltpu.HBM(longer_shape, BF16), jax.ShapeDtypeStruct((2, 8, chans), F32), jax.ShapeDtypeStruct(shape, BF16)],
        scratch_shapes=[
            pltpu.VMEM((2,) + shape, BF16),
            pltpu.VMEM((2, 3, 3, chans, chans), BF16),
            pltpu.VMEM(sums, F32),
            pltpu.VMEM(shape, F32),
            pltpu.VMEM((rows, 2, frames, cols, chans), BF16),
            pltpu.VMEM(longer_shape, BF16),
            DMA((2, 3)),
            DMA,
            DMA,
            DMA((rows,)),
            DMA((frames,)),
        ],
        compiler_params=params(28),
    )(cot, above, below, taps, in_hbm(own_centre), act, gathered, gain, shift)
    pre_grad, pay = pl.pallas_call(
        point_kernel,
        in_specs=[WHOLE] * 6 + [ANY],
        out_specs=[HBM, HBM],
        out_shape=[pltpu.HBM(shape, F32), pltpu.HBM(gathered_shape.shape, F32)],
        scratch_shapes=[
            pltpu.VMEM(shape, F32),
            pltpu.VMEM(shape, BF16),
            pltpu.VMEM(gathered_shape.shape, F32),
            DMA((frames, rows)),
            DMA,
            DMA,
        ],
        cost_estimate=pl.CostEstimate(flops=2 * 10**10, bytes_accessed=10**6, transcendentals=0),
        compiler_params=params(16),
    )(own, incoming, act_held, stats, gain, shift, early)
    gathered = lax.all_to_all(pay, BOTH, 0, 0, tiled=True)
    output, act_late = pl.pallas_call(
        conv_kernel,
        in_specs=[HBM, WHOLE, HBM, WHOLE, WHOLE, WHOLE, HBM],
        out_specs=[WHOLE] * 2,
        out_shape=[jax.ShapeDtypeStruct(shape, BF16)] * 2,
        scratch_shapes=[
            pltpu.VMEM((frames + 2, rows + 2, cols, chans), BF16),
            pltpu.VMEM((frames, rows, cols, 3 * chans), BF16),
            pltpu.VMEM((frames, rows, cols, 6 * chans), BF16),
            pltpu.VMEM((3, 3, chans, chans), BF16),
            pltpu.VMEM((3, 2, 3, chans, chans), BF16),
            pltpu.VMEM(sums, F32),
            DMA,
            DMA((3,)),
            DMA((3,)),
            DMA,
        ],
        compiler_params=params(36),
    )(in_hbm(acts), prior, taps, stats, gain, shift, act)
    output, gathered = lax.optimization_barrier((output, gathered))
    input_grad = pl.pallas_call(
        final_kernel,
        in_specs=[HBM] + [WHOLE] * 4,
        out_specs=HBM,
        out_shape=pltpu.HBM(shape, BF16),
        scratch_shapes=[
            pltpu.VMEM(shape, F32),
            pltpu.VMEM(shape, BF16),
            DMA((frames, rows)),
            DMA((frames, rows)),
        ],
        compiler_params=params(16),
    )(in_hbm(pre_grad), act_late, gathered, stats, gain)
    return (output, input_grad)


def solution(mesh):
    placed = (P("ta", "ha", None, None), P(), P(), P(), P("ta", "ha", None, None))
    return jax.shard_map(
        on_device,
        mesh=mesh,
        in_specs=placed,
        out_specs=(P("ta", "ha", None, None), P("ta", "ha", None, None)),
        check_vma=False,
    )
```

```python
import jax
import jax.numpy as jnp
from jax import lax
from jax.experimental import pallas as pl
from jax.experimental.pallas import tpu as pltpu
from jax.sharding import PartitionSpec as P

GROUPS = 32
LANES = 128
F32 = jnp.float32
BF16 = jnp.bfloat16
HBM = pl.BlockSpec(memory_space=pltpu.HBM)
ANY = pl.BlockSpec(memory_space=pl.ANY)
WHOLE = pl.BlockSpec(memory_space=pltpu.VMEM)
DMA = pltpu.SemaphoreType.DMA
BOTH = ("ta", "ha")


def params(mebibytes):
    return pltpu.CompilerParams(vmem_limit_bytes=mebibytes * 2**20)


def member(chans, across):
    shape, chan_dim = ((LANES, chans), 1) if across else ((chans, LANES), 0)
    per_group = chans // GROUPS
    chan = lax.broadcasted_iota(jnp.int32, shape, chan_dim)
    lane = lax.broadcasted_iota(jnp.int32, shape, 1 - chan_dim)
    inside = (chan >= lane * per_group) & (chan < (lane + 1) * per_group)
    return jnp.where(inside, 1.0, 0.0).astype(BF16)


def exact_dot(left, right):
    high = left.astype(BF16).astype(F32)
    rest = left - high
    middle = rest.astype(BF16).astype(F32)
    parts = jnp.concatenate([high, middle, rest - middle], axis=0).astype(BF16)
    out = jnp.dot(parts, right, preferred_element_type=F32)
    rows = left.shape[0]
    return out[2 * rows :] + out[rows : 2 * rows] + out[:rows]


def to_groups(one, two):
    lanes = exact_dot(jnp.concatenate([one, two], axis=0), member(one.shape[1], False))
    return jnp.sum(lanes[:8] + pltpu.roll(lanes[8:], GROUPS, 1), axis=0, keepdims=True)


def to_chans(one, two, chans):
    rows = jnp.concatenate([jnp.broadcast_to(one, (8, LANES)), jnp.broadcast_to(two, (8, LANES))], axis=0)
    out = exact_dot(rows, member(chans, True))
    return out[:8], out[8:]


def second_part(row):
    return pltpu.roll(jnp.broadcast_to(row, (8, LANES)), LANES - GROUPS, 1)[:1]


def eights(value):
    return value.reshape(value.shape[0] // 8, 8, value.shape[1])


def pack_kernel(act, cot, up, down, sem):
    packs = []
    for n, source in enumerate((act, cot)):
        for k, (h, side) in enumerate(((0, down), (act.shape[1] - 1, up))):
            packs.append(pltpu.make_async_copy(source.at[:, h], side.at[n], sem.at[n, k]))
            packs[-1].start()
    for pack in packs:
        pack.wait()


def stats_kernel(up, down, pay):
    frames, cols, chans = up.shape[1:]
    blocks = [(t, side) for t in range(frames) for side in (down, up)]
    entries = len(blocks) * cols * (chans // GROUPS)
    none = jnp.zeros((8, chans), F32)
    total = none
    for t, side in blocks:
        total = total + jnp.sum(eights(side[0, t].astype(F32)), axis=0)
    sums = to_groups(total, none)
    mean, _ = to_chans(sums / entries, sums, chans)
    spread = none
    for t, side in blocks:
        centered = eights(side[0, t].astype(F32)) - mean[None]
        spread = spread + jnp.sum(centered * centered, axis=0)
    pay[...] = jnp.broadcast_to(sums + to_groups(none, spread), pay.shape)


def centre_kernel(up, down, weight, taps, early, own, block, acc, late, tap_sem, late_sem):
    frames, cols, chans = up.shape[1:]
    rows = 2
    half = rows * cols
    order = [(2, 1), (1, 1), (0, 1), (0, 0), (0, 2), (1, 0), (1, 2)]
    fetches = [pltpu.make_async_copy(weight.at[a, b], taps.at[a, b], tap_sem.at[a, b]) for a, b in order]
    fetches[0].start()
    for t in range(frames):
        block[t, 0] = down[1, t]
        block[t, 1] = up[1, t]
    fetches[1].start()
    left = block[...].reshape(2 * half, chans)
    for n, a in enumerate((2, 1, 0)):
        fetches[n].wait()
        for fetch in (fetches[2:4], fetches[4:6], [])[n]:
            fetch.start()
        for c in (0, 2, 1):
            if a < 2 and c == 1:
                sides(acc.at[a], 2, 0, 2 * rows)
            term = transposed_dot(left, taps[a, 1, c])
            if a == 2:
                acc[1, c] = term
            elif a == 1:
                acc[1, c, :half] += term[half:]
                acc[0, c, half:] = term[:half]
            else:
                acc[0, c, :half] = term[:half]
                acc[0, c, half:] += term[half:]
        if a == 1:
            for fetch in fetches[6:]:
                fetch.start()
            finish(acc.at[1], late, 2, None)
            send = pltpu.make_async_copy(late, own, late_sem)
            send.start()
    finish(acc.at[0], early, 2, None)
    send.wait()
    for fetch in fetches[3:]:
        fetch.wait()


def transposed_dot(left, right):
    return lax.dot_general(left, right, (((1,), (1,)), ((), ())), preferred_element_type=F32)


def grad_products(full, part, source, target, lefts, taps, acc, before=None, between=None):
    half = lefts[0].shape[1] * lefts[0].shape[2]
    chans = lefts[0].shape[3]
    for n, b in enumerate((0, 2)):
        if before is not None:
            before(n)
        both = lefts[n][...].reshape(2 * half, chans)
        one = lefts[n][source].reshape(half, chans)
        for c in (0, 2, 1):
            if b == 2 and c == 1:
                sides(acc, 2, 0, half // lefts[0].shape[2] * 2)
            term = transposed_dot(both, taps[full, b, c])
            if b == 0:
                acc[c] = term
            else:
                acc[c] += term
            if between is not None:
                between(b, c)
            acc[c, target * half : (target + 1) * half] += transposed_dot(one, taps[part, b, c])


def fill_lefts(cot, above, below, lefts):
    for t in range(lefts.shape[1]):
        lefts[0, t, 0] = cot[1][1, t]
        lefts[0, t, 1] = below[1, t]
        lefts[1, t, 0] = above[1, t]
        lefts[1, t, 1] = cot[0][1, t]


def early_kernel(up, down, above, below, taps, centre, out, longer, lefts, acc, send_sem):
    sends = [
        pltpu.make_async_copy(side.at[0, t], longer.at[t, n], send_sem.at[t, n])
        for n, side in enumerate((above, down, up, below))
        for t in range(out.shape[0])
    ]
    for send in sends:
        send.start()
    fill_lefts((down, up), above, below, lefts)
    grad_products(0, 1, 0, 1, (lefts.at[0], lefts.at[1]), taps, acc)
    finish(acc, out, 2, centre)
    for send in sends:
        send.wait()


def activation(mean, rstd, gain, shift, out):
    chans, rows = out.shape[3], out.shape[1]
    gains = jnp.broadcast_to(gain[...], (8, chans))
    shifts = jnp.broadcast_to(shift[...], (8, chans))
    row_at = lax.axis_index("ha")
    last_row = lax.axis_size("ha") - 1
    top = jnp.where(row_at == 0, 0.0, 1.0).astype(F32)
    bottom = jnp.where(row_at == last_row, 0.0, 1.0).astype(F32)

    def activate(values, t, i):
        normed = (eights(values.astype(F32)) - mean[None]) * rstd[None]
        pre = normed * gains[None] + shifts[None]
        value = pre / (1.0 + jnp.exp(-pre))
        if i == 0:
            value = value * top
        if i == rows - 1:
            value = value * bottom
        out[t, i] = value.reshape(values.shape).astype(BF16)

    return activate


def own_kernel(cot, above, below, weight, centre, act, gathered, gain, shift, out, longer, stats, raw, lefts, taps, acc, more, block, acts, tap_sem, more_sem, raw_sem, block_sem, acts_sem):
    frames, rows, cols, chans = act.shape
    load_act = pltpu.make_async_copy(act, raw, raw_sem)
    load_act.start()
    load_cot = [pltpu.make_async_copy(cot.at[:, h], block.at[h, 1], block_sem.at[h]) for h in range(rows)]
    for load in load_cot:
        load.start()
    fetches = [
        [pltpu.make_async_copy(weight.at[a, b], taps.at[a - 1, b], tap_sem.at[a - 1, b]) for a in (2, 1)]
        for b in (0, 2)
    ]
    for fetch in fetches[0]:
        fetch.start()
    load_more = pltpu.make_async_copy(centre, more, more_sem)
    entries = frames * rows * cols * (chans // GROUPS)
    mean, rstd = group_stats(gathered[...], entries, chans)
    stats[0] = mean
    stats[1] = rstd
    activate = activation(mean, rstd, gain, shift, acts)
    for t in range(frames):
        activate(above[0, t], t, 0)
        activate(below[0, t], t, rows + 1)
    load_act.wait()
    for fetch in fetches[1]:
        fetch.start()
    sends = [pltpu.make_async_copy(acts.at[t], longer.at[t], acts_sem.at[t]) for t in range(frames)]
    for load in load_cot:
        load.wait()
    fill_lefts((block.at[0], block.at[1]), above, below, lefts)

    def before(n):
        for fetch in fetches[n]:
            fetch.wait()
        if n == 0:
            load_more.start()
        else:
            for send in sends:
                send.start()

    def between(b, c):
        if b == 0 and c != 1:
            t = 0 if c == 0 else 1
            for h in range(rows):
                activate(raw[t, h], t, 1 + h)

    grad_products(1, 0, 1, 0, (lefts.at[0], lefts.at[1]), taps, acc, before, between)
    load_more.wait()
    finish(acc, out, 2, more)
    for send in sends:
        send.wait()


def sides(acc, earlier, later, frames_rows):
    positions, chans = acc.shape[1:]
    cols = positions // frames_rows
    col = lax.broadcasted_iota(jnp.int32, (cols, chans), 0)
    for n in range(frames_rows):
        at = slice(n * cols, (n + 1) * cols)
        before = jnp.where(col == 0, 0.0, pltpu.roll(acc[earlier, at], 1, 0))
        after = jnp.where(col == cols - 1, 0.0, pltpu.roll(acc[later, at], cols - 1, 0))
        acc[earlier, at] = before + after


def finish(acc, out, beside, more):
    frames, rows, cols, chans = out.shape
    for t in range(frames):
        for h in range(rows):
            at = slice((t * rows + h) * cols, (t * rows + h + 1) * cols)
            total = acc[beside, at] + acc[1, at]
            if more is not None:
                total = total + more[t, h]
            out[t, h] = total.astype(out.dtype)


def group_stats(gathered, entries, chans):
    parts = gathered.shape[0]
    count = parts * entries
    sums = jnp.sum(gathered, axis=0, keepdims=True)
    mean = sums / count
    apart = gathered * (1.0 / entries) - mean
    between = jnp.sum(apart * apart, axis=0, keepdims=True) * entries
    var = (between + second_part(sums)) / count
    lane = lax.broadcasted_iota(jnp.int32, (1, LANES), 1)
    rstd = jnp.where(lane < GROUPS, lax.rsqrt(jnp.where(lane < GROUPS, var, 1.0) + 1e-06), 0.0)
    return to_chans(mean, rstd, chans)


def point_kernel(own, incoming, act, stats, gain, shift, early, pre_grad, pay, block, extra, row_out, block_sem, extra_sem, row_sem):
    frames, rows, cols, chans = act.shape
    mean, rstd = stats[0], stats[1]
    first = lax.axis_index("ta") == 0

    @pl.when(first)
    def _():
        load = pltpu.make_async_copy(early, extra, extra_sem)
        load.start()
        load.wait()
        for h in range(rows):
            block[0, h] = extra[0, h].astype(F32) + extra[1, h].astype(F32)

    @pl.when(jnp.logical_not(first))
    def _():
        block[0] = jnp.zeros_like(block[0])

    gains = jnp.broadcast_to(gain[...], (8, chans))
    shifts = jnp.broadcast_to(shift[...], (8, chans))
    shift_sum = jnp.zeros((8, chans), F32)
    gain_sum = jnp.zeros((8, chans), F32)
    sends = []
    for t in range(frames):
        for h in range(rows):
            grad = own[t, h] + incoming[t, h].astype(F32)
            if t == 0:
                grad = grad + block[0, h]
            normed = (eights(act[t, h].astype(F32)) - mean[None]) * rstd[None]
            pre = normed * gains[None] + shifts[None]
            sig = 1.0 / (1.0 + jnp.exp(-pre))
            local = eights(grad) * sig * (1.0 + pre * (1.0 - sig))
            block[t, h] = local.reshape(cols, chans)
            shift_sum = shift_sum + jnp.sum(local, axis=0)
            gain_sum = gain_sum + jnp.sum(local * normed, axis=0)
            sends.append(pltpu.make_async_copy(block.at[t, h], pre_grad.at[t, h], block_sem.at[t, h]))
            sends[-1].start()
    row = to_groups(gains * shift_sum, gains * gain_sum)
    row_out[...] = jnp.broadcast_to(row, pay.shape)
    sends.append(pltpu.make_async_copy(row_out, pay, row_sem))
    sends[-1].start()
    for send in sends:
        send.wait()


def conv_kernel(acts, prior, weight, stats, gain, shift, act, out, held, ext, near, far, near_taps, far_taps, acc, ext_sem, near_sem, far_sem, held_sem):
    frames, rows, cols, chans = out.shape
    positions = frames * rows * cols
    order = (0, 2, 1)
    first = lax.axis_index("ta") == 0
    own = pltpu.make_async_copy(acts, ext.at[frames:], ext_sem)
    own.start()
    fetches = [pltpu.make_async_copy(weight.at[2, :, c], near_taps.at[c], near_sem.at[c]) for c in order]
    fetches += [pltpu.make_async_copy(weight.at[0:2, :, c], far_taps.at[c], far_sem.at[c]) for c in order]
    fetches[0].start()
    activate = activation(stats[0], stats[1], gain, shift, ext)

    @pl.when(jnp.logical_not(first))
    def _():
        for t in range(frames):
            for i in range(rows + 2):
                activate(prior[t, i], t, i)

    own.wait()
    fetches[1].start()
    fetches[2].start()

    @pl.when(first)
    def _():
        for t in range(frames):
            ext[t] = ext[frames]

    for b in range(3):
        near[:, :, :, b * chans : (b + 1) * chans] = ext[2 : 2 + frames, b : b + rows]
    left = near[...].reshape(positions, 3 * chans)
    for n, c in enumerate(order):
        if n == 0:
            fetches[0].wait()
            fetches[3].start()
        if n == 1:
            fetches[1].wait()
            fetches[2].wait()
            fetches[4].start()
            fetches[5].start()
        acc[c] = jnp.dot(left, near_taps[c].reshape(3 * chans, chans), preferred_element_type=F32)
    for a in range(2):
        for b in range(3):
            k = (3 * a + b) * chans
            far[:, :, :, k : k + chans] = ext[a : a + frames, b : b + rows]
    left = far[...].reshape(positions, 6 * chans)
    for n, c in enumerate(order):
        if n == 0:
            fetches[3].wait()
            hold = pltpu.make_async_copy(act, held, held_sem)
            hold.start()
        if n == 1:
            fetches[4].wait()
            fetches[5].wait()
        if c == 1:
            sides(acc, 0, 2, frames * rows)
        acc[c] += jnp.dot(left, far_taps[c].reshape(6 * chans, chans), preferred_element_type=F32)
    finish(acc, out, 0, None)
    hold.wait()


def final_kernel(pre_grad, act, gathered, stats, gain, out, block, done, block_sem, done_sem):
    frames, rows, cols, chans = act.shape
    places = [(t, h) for t in range(frames) for h in range(rows)]
    loads = [pltpu.make_async_copy(pre_grad.at[at], block.at[at], block_sem.at[at]) for at in places]
    for load in loads:
        load.start()
    count = gathered.shape[0] * frames * rows * cols * (chans // GROUPS)
    sums = jnp.sum(gathered[...], axis=0, keepdims=True) / count
    first, second = to_chans(sums, second_part(sums), chans)
    mean, rstd = stats[0], stats[1]
    gains = jnp.broadcast_to(gain[...], (8, chans))
    sends = []
    for at, load in zip(places, loads):
        load.wait()
        normed = (eights(act[at].astype(F32)) - mean[None]) * rstd[None]
        value = rstd[None] * (eights(block[at]) * gains[None] - first[None] - normed * second[None])
        done[at] = value.reshape(cols, chans).astype(BF16)
        sends.append(pltpu.make_async_copy(done.at[at], out.at[at], done_sem.at[at]))
        sends[-1].start()
    for send in sends:
        send.wait()


def moved(value, frame_step, row_step):
    frames, rows = lax.axis_size("ta"), lax.axis_size("ha")
    pairs = []
    for t in range(frames):
        for h in range(rows):
            to_t, to_h = t + frame_step, h + row_step
            if 0 <= to_t < frames and 0 <= to_h < rows:
                pairs.append((t * rows + h, to_t * rows + to_h))
    return lax.ppermute(value, BOTH, pairs)


def in_hbm(value):
    return pltpu.with_memory_space_constraint(value, pltpu.HBM)


def in_vmem(value):
    return pltpu.with_memory_space_constraint(value, pltpu.VMEM)


def on_device(activations, gain, shift, weight, cotangent):
    shape = activations.shape
    frames, rows, cols, chans = shape
    act, cot, taps = in_hbm(activations), in_hbm(cotangent), in_hbm(weight)
    parts = lax.axis_size("ta") * lax.axis_size("ha")
    gain, shift = gain.reshape(1, chans), shift.reshape(1, chans)
    gathered_shape = jax.ShapeDtypeStruct((parts, LANES), F32)
    edge = jax.ShapeDtypeStruct((2, frames, cols, chans), BF16)
    longer_shape = (frames, rows + 2, cols, chans)
    positions = frames * rows * cols

    up, down = pl.pallas_call(
        pack_kernel,
        in_specs=[HBM, HBM],
        out_specs=[WHOLE] * 2,
        out_shape=[edge, edge],
        scratch_shapes=[DMA((2, 2))],
        compiler_params=params(16),
    )(act, cot)
    pay = pl.pallas_call(
        stats_kernel,
        in_specs=[WHOLE] * 2,
        out_specs=WHOLE,
        out_shape=gathered_shape,
        compiler_params=params(16),
    )(up, down)
    above = moved(up, 0, 1)
    below = moved(down, 0, -1)
    gathered = lax.all_to_all(pay, BOTH, 0, 0, tiled=True)

    f32_block = jax.ShapeDtypeStruct(shape, F32)
    sums = (3, positions, chans)
    held, early_centre, own_centre = pl.pallas_call(
        centre_kernel,
        in_specs=[WHOLE, WHOLE, HBM],
        out_specs=[WHOLE, WHOLE, HBM],
        out_shape=[pltpu.VMEM(weight.shape, BF16), f32_block, pltpu.HBM(shape, F32)],
        scratch_shapes=[
            pltpu.VMEM(shape, BF16),
            pltpu.VMEM((2,) + sums, F32),
            pltpu.VMEM(shape, F32),
            DMA((3, 3)),
            DMA,
        ],
        compiler_params=params(16),
    )(up, down, taps)
    held = in_vmem(held)
    early, longer = pl.pallas_call(
        early_kernel,
        in_specs=[WHOLE] * 6,
        out_specs=[WHOLE, HBM],
        out_shape=[pltpu.VMEM(shape, BF16), pltpu.HBM(longer_shape, BF16)],
        scratch_shapes=[pltpu.VMEM((2,) + shape, BF16), pltpu.VMEM(sums, F32), DMA((frames, rows + 2))],
        compiler_params=params(16),
    )(up, down, above, below, held, early_centre)
    early, gathered = lax.optimization_barrier((early, gathered))
    incoming = moved(early, -1, 0)
    prior = moved(longer, 1, 0)
    own, acts, stats, act_held = pl.pallas_call(
        own_kernel,
        in_specs=[HBM, WHOLE, WHOLE, HBM, HBM, HBM, WHOLE, WHOLE, WHOLE],
        out_specs=[WHOLE, HBM, WHOLE, WHOLE],
        out_shape=[f32_block, pltpu.HBM(longer_shape, BF16), jax.ShapeDtypeStruct((2, 8, chans), F32), jax.ShapeDtypeStruct(shape, BF16)],
        scratch_shapes=[
            pltpu.VMEM((2,) + shape, BF16),
            pltpu.VMEM((2, 3, 3, chans, chans), BF16),
            pltpu.VMEM(sums, F32),
            pltpu.VMEM(shape, F32),
            pltpu.VMEM((rows, 2, frames, cols, chans), BF16),
            pltpu.VMEM(longer_shape, BF16),
            DMA((2, 3)),
            DMA,
            DMA,
            DMA((rows,)),
            DMA((frames,)),
        ],
        compiler_params=params(28),
    )(cot, above, below, taps, in_hbm(own_centre), act, gathered, gain, shift)
    pre_grad, pay = pl.pallas_call(
        point_kernel,
        in_specs=[WHOLE] * 6 + [ANY],
        out_specs=[HBM, HBM],
        out_shape=[pltpu.HBM(shape, F32), pltpu.HBM(gathered_shape.shape, F32)],
        scratch_shapes=[
            pltpu.VMEM(shape, F32),
            pltpu.VMEM(shape, BF16),
            pltpu.VMEM(gathered_shape.shape, F32),
            DMA((frames, rows)),
            DMA,
            DMA,
        ],
        cost_estimate=pl.CostEstimate(flops=2 * 10**10, bytes_accessed=10**6, transcendentals=0),
        compiler_params=params(16),
    )(own, incoming, act_held, stats, gain, shift, early)
    gathered = lax.all_to_all(pay, BOTH, 0, 0, tiled=True)
    output, act_late = pl.pallas_call(
        conv_kernel,
        in_specs=[HBM, WHOLE, HBM, WHOLE, WHOLE, WHOLE, HBM],
        out_specs=[WHOLE] * 2,
        out_shape=[jax.ShapeDtypeStruct(shape, BF16)] * 2,
        scratch_shapes=[
            pltpu.VMEM((frames + 2, rows + 2, cols, chans), BF16),
            pltpu.VMEM((frames, rows, cols, 3 * chans), BF16),
            pltpu.VMEM((frames, rows, cols, 6 * chans), BF16),
            pltpu.VMEM((3, 3, chans, chans), BF16),
            pltpu.VMEM((3, 2, 3, chans, chans), BF16),
            pltpu.VMEM(sums, F32),
            DMA,
            DMA((3,)),
            DMA((3,)),
            DMA,
        ],
        compiler_params=params(36),
    )(in_hbm(acts), prior, taps, stats, gain, shift, act)
    output, gathered = lax.optimization_barrier((output, gathered))
    input_grad = pl.pallas_call(
        final_kernel,
        in_specs=[HBM] + [WHOLE] * 4,
        out_specs=HBM,
        out_shape=pltpu.HBM(shape, BF16),
        scratch_shapes=[
            pltpu.VMEM(shape, F32),
            pltpu.VMEM(shape, BF16),
            DMA((frames, rows)),
            DMA((frames, rows)),
        ],
        compiler_params=params(16),
    )(in_hbm(pre_grad), act_late, gathered, stats, gain)
    return (output, input_grad)


def solution(mesh):
    placed = (P("ta", "ha", None, None), P(), P(), P(), P("ta", "ha", None, None))
    return jax.shard_map(
        on_device,
        mesh=mesh,
        in_specs=placed,
        out_specs=(P("ta", "ha", None, None), P("ta", "ha", None, None)),
        check_vma=False,
    )
```
